32 devices in a mesh: ens: 2 (over x), lat: 16 (over z, y, core).
Axes of the slice: x: 2, y: 2, z: 4, core: 2. Of those that a mesh axis runs over, the one named last changes fastest.
Arguments:
- atmos: bfloat16 [11520, 1024], P(('ens', 'lat')), parts along dimension 0, may hold values from -6 to 6
- ocean_state: bfloat16 [76, 128, 1440], P(None, ('ens', 'lat')), parts along dimension 1, may hold values from -6 to 6
- land_mask: int32 [64, 1440], P('lat'), may hold values 0 or 1
- w_qkv: bfloat16 [1024, 3072], replicated, may hold values from -0.1875 to 0.1875
- w_out: bfloat16 [1024, 1024], replicated, may hold values from -0.1875 to 0.1875
- head_scale: float32 [16], replicated, may hold values from 0.5 to 80
- gain_attn: float32 [1024], replicated, may hold values from 0.5 to 1.5
- gain_flux: float32 [1024], replicated, may hold values from 0.1 to 1.9
- w_flux: bfloat16 [1024, 16], replicated, may hold values from -0.1875 to 0.1875
- surf_embed: float32 [4, 1024], replicated, may hold values from -3 to 3
- flux_start: int32 [64], P('lat'), may hold values from 0 to 14, as said below
- flux_weight: float32 [64, 2], P('lat'), may hold values from 0.25 to 1
- surf_start: int32 [16], P('lat'), may hold values from -2 to 59, as said below
- surf_weight: float32 [16, 7], P('lat'), may hold values from 0.1 to 0.5
- conv_first: bfloat16 [9, 128, 92], replicated, may hold values from -0.21875 to 0.21875
- conv_second: bfloat16 [9, 76, 128], replicated, may hold values from -0.1875 to 0.1875
Outputs:
- atmos_next: bfloat16 [11520, 1024], P(('ens', 'lat')), parts along dimension 0
- ocean_next: bfloat16 [76, 128, 1440], P(None, ('ens', 'lat')), parts along dimension 1
The draws below stay inside these ranges and needn't reach their ends.
There are 2 independent parts, one for each index of `ens`. The reference program is written for one: setup_inputs(seed, part) draws one part's arguments, and reference() takes and returns one part's arrays. A program takes and returns all parts, laid end to end along the dimension named above; an argument that names none is the same for every part. Nothing has to cross between parts.
Inputs may be any that keep to these rules, and one draw needn't show every extreme that they name: flux_start[i] is i // 4 - 1 or i // 4, kept within 0 to 14. surf_start[r] is 4 r - 2 or 4 r - 1.
All inputs are finite; a program needn't handle non-finite values. No bound on the sum of `land_mask` on one device may be relied on, other than what follows from the above.
Results may differ from the reference program's by a relative error of at most 0.0065.
The reference program's roundings to bfloat16 on the way count: a program that leaves them out, or rounds other values in their place, can miss the bound.
Values may be sent and summed in bfloat16 or wider, within the bound.
No kernel may reach another device: no remote copies, remote signals or barrier semaphores. Data moves between devices by JAX's collectives and lax.ppermute only.
A program may use at most 128 MiB of HBM per device.

```python
import jax
import jax.numpy as jnp
from jax import lax

D = 1024
HEADS = 16
NFLUX = 16
LEVELS = 19
VARS = 4
OCH = 76
HID = 128
ALON = 360
SPAN = 4
OLON = 1440
RATIO = 4
AROWS = 16
OROWS = 64
TOKENS = 5760
FBAND = 2
OBAND = 7
OSTEPS = 2


def draw_head_scale(key, part):
    lowest = jnp.log(jnp.float32(0.5))
    highest = jnp.log(jnp.float32(2.5))
    moderate = jnp.exp(jax.random.uniform(key, (HEADS,), jnp.float32, lowest, highest))
    return moderate


def draw_flux_start(key, part):
    ocean_rows = jnp.arange(OROWS, dtype=jnp.int32)
    jitter = jax.random.randint(key, (OROWS,), 0, 2, dtype=jnp.int32)
    return jnp.clip(ocean_rows // RATIO - 1 + jitter, 0, AROWS - FBAND).astype(jnp.int32)


def draw_surf_start(key, part):
    centres = jnp.arange(AROWS, dtype=jnp.int32) * RATIO
    jitter = jax.random.randint(key, (AROWS,), 0, 2, dtype=jnp.int32)
    return (centres - 2 + jitter).astype(jnp.int32)


def touch_ends(entries, rng, least, top_value):
    place = [jax.random.randint(jax.random.fold_in(rng, axis), (), 0, length) for axis, length in enumerate(entries.shape)]
    widest = entries.shape.index(max(entries.shape))
    beside = place[:widest] + [(place[widest] + 1) % entries.shape[widest]] + place[widest + 1:]
    return entries.at[tuple(place)].set(least).at[tuple(beside)].set(top_value)


def block_scale(rng, shape, cuts, smallest, top_value):
    loudness = 1.0
    for axis_at, shards_of in cuts:
        draws = jax.random.uniform(jax.random.fold_in(jax.random.fold_in(rng, 6), axis_at), (shards_of,), jnp.float32, smallest / len(cuts), top_value / len(cuts))
        loudness = loudness * jnp.repeat(jnp.exp(draws), shape[axis_at] // shards_of).reshape((-1,) + (1,) * (len(shape) - 1 - axis_at))
    return loudness


def bell_draw(stream_key, dims, scale, most, shards=(), held_as=jnp.bfloat16):
    loudness = block_scale(stream_key, dims, shards, -0.22, 0.18) if shards else 1.0
    entries = jax.random.normal(stream_key, dims, jnp.float32) * scale * loudness
    return jnp.minimum(jnp.maximum(entries, -most), most).astype(held_as)


def setup_inputs(seed: int = 0, part: int = 0) -> dict:
    seeds = jax.random.split(jax.random.key(seed), 17)
    part_splits = jax.random.split(jax.random.fold_in(seeds[16], part), 17)
    return {
        "atmos": bell_draw(part_splits[0], (TOKENS, D), 1.0, 6.0, ((0, 16),)),
        "ocean_state": bell_draw(part_splits[1], (OCH, OROWS, OLON), 1.0, 6.0, ((1, 16),)),
        "land_mask": touch_ends((jax.random.randint(seeds[2], (OROWS, OLON), 0, 10) < 7).astype(jnp.int32), jax.random.fold_in(seeds[2], 1), 0, 1),
        "w_qkv": bell_draw(seeds[3], (D, 3 * D), D ** -0.5, 0.1875),
        "w_out": bell_draw(seeds[4], (D, D), D ** -0.5, 0.1875),
        "head_scale": draw_head_scale(jax.random.fold_in(seeds[16], 71), part),
        "gain_attn": jnp.clip(1.0 + 0.1 * jax.random.normal(seeds[6], (D,), jnp.float32), 0.5, 1.5),
        "gain_flux": jnp.clip(1.0 + 0.18 * jax.random.normal(seeds[7], (D,), jnp.float32), 0.1, 1.9),
        "w_flux": bell_draw(seeds[8], (D, NFLUX), D ** -0.5, 0.1875),
        "surf_embed": bell_draw(seeds[9], (VARS, D), VARS ** -0.5, 3.0, (), jnp.float32),
        "flux_start": draw_flux_start(jax.random.fold_in(seeds[16], 71), part),
        "flux_weight": jnp.clip(0.25 + 0.75 * jax.random.uniform(seeds[11], (OROWS, FBAND), jnp.float32) ** block_scale(seeds[11], (OROWS, FBAND), ((0, 16),), -0.2, 0.2), 0.25, 1.0),
        "surf_start": draw_surf_start(jax.random.fold_in(seeds[16], 71), part),
        "surf_weight": jnp.clip(0.1 + 0.4 * jax.random.uniform(seeds[13], (AROWS, OBAND), jnp.float32) ** block_scale(seeds[13], (AROWS, OBAND), ((0, 16),), -0.2, 0.2), 0.1, 0.5),
        "conv_first": bell_draw(seeds[14], (9, HID, OCH + NFLUX), (9 * (OCH + NFLUX)) ** -0.5, 0.21875),
        "conv_second": bell_draw(seeds[15], (9, OCH, HID), (9 * HID) ** -0.5, 0.1875),
    }


def rms_norm(values, scaling):
    return values * lax.rsqrt(lax.optimization_barrier(jnp.mean(values * values, axis=-1, keepdims=True)) + 1e-06) * scaling

def band_matrix(starts, weight, first_col, col_count):
    columns = first_col + jnp.arange(col_count, dtype=jnp.int32)
    summed = jnp.zeros((starts.shape[0], col_count), jnp.float32)
    for offset in range(weight.shape[1]):
        matches = (columns[None, :] == starts[:, None] + offset).astype(jnp.float32)
        summed = summed + weight[:, offset:offset + 1] * matches
    return summed

def surface_rows(ocean_now):
    fields = ocean_now[0::LEVELS]
    averaged = lax.optimization_barrier(jnp.mean(fields.reshape(fields.shape[0], fields.shape[1], fields.shape[2] // SPAN, SPAN), axis=3))
    return averaged.transpose(1, 0, 2).reshape(fields.shape[1], -1)

def head_parts(qkv, head_scale):
    token_count = qkv.shape[0]
    width = qkv.shape[1] // 3
    head_count = head_scale.shape[0]
    depth = width // head_count
    query_raw = qkv[:, :width].reshape(token_count, head_count, depth)
    key_raw = qkv[:, width:2 * width].reshape(token_count, head_count, depth)
    query_part = query_raw * lax.rsqrt(lax.optimization_barrier(jnp.mean(query_raw * query_raw, axis=-1, keepdims=True)) + 1e-06)
    query_part = query_part * (head_scale[None, :, None] / jnp.sqrt(jnp.float32(depth)))
    key_part = key_raw * lax.rsqrt(lax.optimization_barrier(jnp.mean(key_raw * key_raw, axis=-1, keepdims=True)) + 1e-06)
    value_part = qkv[:, 2 * width:]
    return (query_part.astype(jnp.bfloat16), key_part.astype(jnp.bfloat16), value_part.astype(jnp.bfloat16))

def attend(query_rows, key_rows, value_rows, valid):
    key_count = key_rows.shape[0]
    scores = jnp.einsum('qhd,khd->hqk', query_rows.astype(jnp.float32), key_rows.astype(jnp.float32))
    scores = jnp.where(valid[None, None, :], scores, -1e+30)
    largest = lax.optimization_barrier(jnp.max(scores, axis=2, keepdims=True))
    raised = jnp.exp(scores - largest)
    probs = (raised / lax.optimization_barrier(jnp.sum(raised, axis=2, keepdims=True))).astype(jnp.bfloat16)
    value_heads = value_rows.reshape(key_count, key_rows.shape[1], key_rows.shape[2])
    mixed = jnp.einsum('hqk,khd->qhd', probs.astype(jnp.float32), value_heads.astype(jnp.float32))
    return mixed.astype(jnp.bfloat16).reshape(query_rows.shape[0], -1)

def spread_flux(regridded, flux_count):
    row_count = regridded.shape[0]
    shaped = regridded.reshape(row_count, -1, flux_count).transpose(2, 0, 1)
    return jnp.repeat(shaped, SPAN, axis=2).astype(jnp.bfloat16)

def convolve(padded, weight, row_count):
    channels = padded.shape[0]
    lon_count = padded.shape[2]
    summed = jnp.zeros((weight.shape[1], row_count * lon_count), jnp.float32)
    for tap_index in range(9):
        row_step = tap_index // 3 - 1
        lon_step = tap_index % 3 - 1
        shifted = jnp.roll(padded[:, 1 + row_step:1 + row_step + row_count, :], -lon_step, axis=2)
        summed = summed + jnp.dot(weight[tap_index], shifted.reshape(channels, -1), preferred_element_type=jnp.float32)
    return summed.reshape(weight.shape[1], row_count, lon_count)

def pad_rows(fields):
    return jnp.pad(fields, ((0, 0), (1, 1), (0, 0)))

def reference(atmos, ocean_state, land_mask, w_qkv, w_out, head_scale, gain_attn, gain_flux, w_flux, surf_embed, flux_start, flux_weight, surf_start, surf_weight, conv_first, conv_second):
    ocean_now = ocean_state.astype(jnp.float32)
    surface = surface_rows(ocean_now).astype(jnp.bfloat16)
    surf_matrix = band_matrix(surf_start, surf_weight, 0, OROWS)
    surf_atm = jnp.dot(surf_matrix, surface.astype(jnp.float32), precision=lax.Precision.HIGHEST)
    surf_tokens = surf_atm.reshape(AROWS, VARS, ALON).transpose(0, 2, 1).reshape(AROWS * ALON, VARS)
    start = atmos.astype(jnp.float32) + jnp.dot(surf_tokens, surf_embed, precision=lax.Precision.HIGHEST)
    normed = rms_norm(start, gain_attn).astype(jnp.bfloat16)
    qkv = jnp.dot(normed, w_qkv, preferred_element_type=jnp.float32)
    query_part, key_part, value_part = head_parts(qkv, head_scale)
    head_count = query_part.shape[1]
    depth = query_part.shape[2]
    query_grid = query_part.reshape(AROWS, ALON, head_count, depth)
    key_grid = jnp.pad(key_part.reshape(AROWS, ALON, head_count, depth), ((1, 1), (0, 0), (0, 0), (0, 0)))
    value_grid = jnp.pad(value_part.reshape(AROWS, ALON, D), ((1, 1), (0, 0), (0, 0)))

    def one_row(row_id):
        query_rows = lax.dynamic_slice_in_dim(query_grid, row_id, 1, 0)[0]
        key_rows = lax.dynamic_slice_in_dim(key_grid, row_id, 3, 0).reshape(3 * ALON, head_count, depth)
        value_rows = lax.dynamic_slice_in_dim(value_grid, row_id, 3, 0).reshape(3 * ALON, D)
        global_rows = row_id - 1 + jnp.arange(3 * ALON, dtype=jnp.int32) // ALON
        valid = (global_rows >= 0) & (global_rows < AROWS)
        return attend(query_rows, key_rows, value_rows, valid)
    mixed = lax.map(one_row, jnp.arange(AROWS, dtype=jnp.int32)).reshape(AROWS * ALON, D)
    after = start + jnp.dot(mixed, w_out, preferred_element_type=jnp.float32)
    atmos_next = after.astype(jnp.bfloat16)
    flux_in = rms_norm(after, gain_flux).astype(jnp.bfloat16)
    fluxes = jnp.dot(flux_in, w_flux, preferred_element_type=jnp.float32).astype(jnp.bfloat16).reshape(AROWS, ALON * NFLUX)
    flux_matrix = band_matrix(flux_start, flux_weight, 0, AROWS)
    regridded = jnp.dot(flux_matrix, fluxes.astype(jnp.float32), precision=lax.Precision.HIGHEST)
    ocean_flux = spread_flux(regridded, NFLUX)
    sea_cells = land_mask.astype(jnp.float32)
    for step_index in range(OSTEPS):
        inputs = jnp.concatenate([ocean_now.astype(jnp.bfloat16), ocean_flux], axis=0)
        hidden = jax.nn.gelu(convolve(pad_rows(inputs), conv_first, OROWS), approximate=True).astype(jnp.bfloat16)
        ocean_now = ocean_now + sea_cells[None] * convolve(pad_rows(hidden), conv_second, OROWS)
    return (atmos_next, ocean_now.astype(jnp.bfloat16))
```

```python
import functools

import jax
import jax.numpy as jnp
from jax import lax
from jax.experimental import pallas as pl
from jax.experimental.pallas import tpu as pltpu
from jax.sharding import PartitionSpec as P

LEVELS = 19
VARS = 4
SPAN = 4
LANE = 128
F32 = jnp.float32
BF16 = jnp.bfloat16
VMEM = pl.BlockSpec(memory_space=pltpu.VMEM)
SMEM = pl.BlockSpec(memory_space=pltpu.SMEM)
PARAMS = pltpu.CompilerParams(vmem_limit_bytes=58 * 2**20)


def cost(flops, size):
    return pl.CostEstimate(flops=int(flops), bytes_accessed=int(size), transcendentals=0)


def up_to(value, unit):
    return (value + unit - 1) // unit * unit


def iota(shape, axis):
    return lax.broadcasted_iota(jnp.int32, shape, axis)


def swap_in_chip(block):
    count = lax.axis_size("lat")
    return lax.ppermute(block, "lat", [(i, i ^ 1) for i in range(count)])


def swap_across(block):
    count = lax.axis_size("lat")
    pairs = []
    for i in range(1, count - 1, 2):
        pairs += [(i, i + 1), (i + 1, i)]
    return lax.ppermute(block, "lat", pairs)


def split3(values):
    high = values.astype(BF16)
    rest = values - high.astype(F32)
    middle = rest.astype(BF16)
    low = (rest - middle.astype(F32)).astype(BF16)
    return high, middle, low


def surface_kernel(pos_ref, sstart_ref, fstart_ref, sw_ref, fw_ref, *refs):
    fields = refs[:VARS]
    out_ref, tile = refs[VARS], refs[VARS + 1]
    orows, olon = fields[0].shape[1:]
    wide = SPAN * LANE
    parts = jnp.concatenate([f[0].astype(F32) for f in fields], axis=0).astype(BF16)
    gather = jnp.where(iota((wide, LANE), 0) // SPAN == iota((wide, LANE), 1), 1.0 / SPAN, 0.0)
    gather = gather.astype(BF16)
    tile[...] = jnp.zeros_like(tile)
    for at in range(0, olon, wide):
        size = min(wide, olon - at)
        tile[0:16, at // SPAN : at // SPAN + LANE] = jnp.dot(
            parts[:, at : at + size], gather[:size], preferred_element_type=F32
        )
    weights = sw_ref.shape[1]
    for index, piece in enumerate(split3(sw_ref[...])):
        tile[16 + index : 17 + index, 0:weights] = piece.astype(F32)
    position = pos_ref[0]
    tile[19:20, 0:LANE] = jnp.full((1, LANE), 1.0, F32) * (
        sstart_ref[0] - position * orows
    ).astype(F32)
    for index, piece in enumerate(split3(fw_ref[...])):
        tile[20 + 4 * index : 24 + 4 * index, 0 : fw_ref.shape[1]] = piece.astype(F32)
    lanes = iota((1, LANE), 1)
    for row in range(orows):
        start = (fstart_ref[row] - position).astype(F32)
        tile[20 + row : 21 + row, 0:LANE] = jnp.where(
            lanes == 2, start, tile[20 + row : 21 + row, 0:LANE]
        )
    out_ref[...] = tile[...].astype(BF16)


def surface_message(pos, ocean_state, surf_start, surf_weight, flux_start, flux_weight):
    channels, orows, olon = ocean_state.shape
    width = up_to(olon // SPAN, LANE)
    specs = [
        pl.BlockSpec((1, orows, olon), functools.partial(lambda v, i: (v * LEVELS, 0, 0), v))
        for v in range(VARS)
    ]
    return pl.pallas_call(
        surface_kernel,
        out_shape=jax.ShapeDtypeStruct((32, width), BF16),
        grid=(1,),
        in_specs=[SMEM, SMEM, SMEM, VMEM, VMEM] + specs,
        out_specs=pl.BlockSpec((32, width), lambda i: (0, 0)),
        scratch_shapes=[pltpu.VMEM((32, width), F32)],
        compiler_params=PARAMS,
        cost_estimate=cost(1e6, 1e5),
        name="surface",
    )(pos, surf_start, flux_start, surf_weight, flux_weight, *([ocean_state] * VARS))


def relayout_kernel(ocean_ref, mask_ref, out_ref, wide, row_ref):
    channels, orows, olon = ocean_ref.shape
    width = out_ref.shape[2]
    wide[...] = ocean_ref[...].astype(F32)
    row_ref[...] = jnp.zeros_like(row_ref)
    pad = width - olon
    lanes = iota((1, width), 1)
    for row in range(orows):
        row_ref[0:channels, 0:olon] = wide[:, row, :]
        row_ref[channels : channels + 1, 0:olon] = mask_ref[row : row + 1, :].astype(F32)
        values = row_ref[...]
        ahead = pltpu.roll(values, olon, 1)
        behind = pltpu.roll(values, pad, 1)
        values = jnp.where((lanes >= olon) & (lanes < olon + SPAN), ahead, values)
        values = jnp.where(lanes >= width - SPAN, behind, values)
        out_ref[row] = values.astype(BF16)


def relayout(ocean_state, land_mask):
    channels, orows, olon = ocean_state.shape
    width = up_to(olon + 2 * SPAN, LANE)
    deep = up_to(channels + 1, 16)
    return pl.pallas_call(
        relayout_kernel,
        out_shape=jax.ShapeDtypeStruct((orows, deep, width), BF16),
        in_specs=[VMEM, VMEM],
        out_specs=VMEM,
        scratch_shapes=[pltpu.VMEM((channels, orows, olon), F32), pltpu.VMEM((deep, width), F32)],
        compiler_params=PARAMS,
        cost_estimate=cost(1e7, 4e6),
        name="relayout",
    )(ocean_state, land_mask)


def head_norm(block):
    side = 256
    ones = jnp.where(iota((side, side), 0) // 64 == iota((side, side), 1) // 64, 1.0, 0.0)
    ones = ones.astype(BF16)
    out = []
    for at in range(0, block.shape[1], side):
        part = block[:, at : at + side]
        square = part * part
        high = square.astype(BF16)
        low = (square - high.astype(F32)).astype(BF16)
        total = jnp.dot(high, ones, preferred_element_type=F32)
        total = total + jnp.dot(low, ones, preferred_element_type=F32)
        out.append(part * lax.rsqrt(total * (1.0 / 64) + 1e-06))
    return jnp.concatenate(out, axis=1)


def tokens_start(atmos, embed, sfields, params, orows):
    starts = params[19:20, 0:1].astype(F32)
    weights = (
        params[16:17].astype(F32) + params[17:18].astype(F32) + params[18:19].astype(F32)
    )[:, 0:LANE]
    rows = iota((16, LANE), 0) % orows
    lanes = iota((16, LANE), 1)
    total = None
    for block, fields in zip((-1, 0, 1), sfields):
        place = rows + block * orows - starts.astype(jnp.int32)
        coef = jnp.sum(jnp.where(lanes == place, weights, 0.0), axis=1, keepdims=True)
        term = coef * fields[0:16].astype(F32)
        total = term if total is None else total + term
    a = split3(total)
    rep = jnp.concatenate(
        [jnp.broadcast_to(embed[v : v + 1], (orows, embed.shape[1])) for v in range(VARS)], axis=0
    )
    b = split3(rep)
    left = jnp.concatenate([a[0], a[0], a[0], a[1], a[1], a[2]], axis=0)
    right = jnp.concatenate([b[0], b[1], b[2], b[0], b[1], b[0]], axis=0)
    added = lax.dot_general(left, right, (((0,), (0,)), ((), ())), preferred_element_type=F32)
    return atmos.astype(F32) + added[: atmos.shape[0]]


def project_kernel(first, qsteps, orows, pos_ref, atmos_ref, m0, m1, m2, embed_ref, gain_ref, scale_ref, w_ref, *refs):
    outs, normed = refs[:-1], refs[-1]
    step = pl.program_id(0) + first

    @pl.when(step == first)
    def _():
        start = tokens_start(
            atmos_ref[...], embed_ref[...], (m0[...], m1[...], m2[...]), m1[...], orows
        )
        mean = jnp.mean(start * start, axis=1, keepdims=True)
        normed[...] = (start * lax.rsqrt(mean + 1e-06) * gain_ref[...]).astype(BF16)
        if first == 0:
            outs[0][...] = start

    kv_ref = outs[-1]
    if first == 0:

        @pl.when(step < qsteps)
        def _():
            block = jnp.dot(normed[...], w_ref[...], preferred_element_type=F32)
            outs[1][...] = (head_norm(block) * scale_ref[...]).astype(BF16)

    @pl.when((step >= qsteps) & (step < 2 * qsteps))
    def _():
        block = jnp.dot(normed[...], w_ref[...], preferred_element_type=F32)
        kv_ref[...] = head_norm(block).astype(BF16)

    @pl.when(step >= 2 * qsteps)
    def _():
        block = jnp.dot(normed[...], w_ref[...], preferred_element_type=F32)
        kv_ref[...] = block.astype(BF16)


def project(pos, atmos, messages, surf_embed, gain, scale, w_qkv, orows, with_query):
    tokens, width = atmos.shape
    side = 512
    qsteps = width // side
    first = 0 if with_query else qsteps
    kv_out = jax.ShapeDtypeStruct((tokens, 2 * width), BF16)
    kv_spec = pl.BlockSpec((tokens, side), lambda j: (0, jnp.maximum(j + first - qsteps, 0)))
    whole = pl.BlockSpec((tokens, width), lambda j: (0, 0))
    if with_query:
        out_shape = (
            jax.ShapeDtypeStruct((tokens, width), F32),
            jax.ShapeDtypeStruct((tokens, width), BF16),
            kv_out,
        )
        q_spec = pl.BlockSpec((tokens, side), lambda j: (0, jnp.minimum(j, qsteps - 1)))
        out_specs = (whole, q_spec, kv_spec)
    else:
        out_shape, out_specs = (kv_out,), (kv_spec,)
    return pl.pallas_call(
        functools.partial(project_kernel, first, qsteps, orows),
        out_shape=out_shape,
        grid=(3 * qsteps - first,),
        in_specs=[SMEM, VMEM, VMEM, VMEM, VMEM, VMEM, VMEM]
        + [
            pl.BlockSpec((1, side), lambda j: (0, jnp.minimum(j, qsteps - 1))),
            pl.BlockSpec((width, side), lambda j: (0, j + first)),
        ],
        out_specs=out_specs,
        scratch_shapes=[pltpu.VMEM((tokens, width), BF16)],
        compiler_params=PARAMS,
        cost_estimate=cost(2 * tokens * width * width * (3 if with_query else 2), 8e6),
        name="project",
    )(pos, atmos, *messages, surf_embed, gain, scale, w_qkv)


def attend_kernel(per, pos_ref, q_ref, k0, v0, k1, v1, k2, v2, wo_ref, start_ref, gain_ref, wf_ref, next_ref, flux_ref, total):
    step = pl.program_id(0)
    rows = q_ref.shape[0]
    wide = q_ref.shape[1]
    depth = wide // per
    position, count = pos_ref[0], pos_ref[1]
    exists = ((position > 0) | (position % 2 == 1)) & (
        (position < count - 1) | (position % 2 == 0)
    )
    penalty = jnp.where(exists, 0.0, 1e30).astype(F32)
    keys = (k0[...], k1[...], k2[...])
    values = (v0[...], v1[...], v2[...])
    query = q_ref[...]
    lanes = iota((1, wide), 1) // depth
    mixed = jnp.zeros((rows, wide), F32)
    for head in range(per):
        mine = jnp.where(lanes == head, query, jnp.zeros_like(query))
        scores = [
            lax.dot_general(mine, key, (((1,), (1,)), ((), ())), preferred_element_type=F32)
            for key in keys
        ]
        tops = [jnp.max(s, axis=1, keepdims=True) for s in scores]
        top = jnp.maximum(jnp.maximum(tops[0], tops[1]), tops[2] - penalty)
        shift = (top, top, top + penalty)
        raised = [jnp.exp(s - m) for s, m in zip(scores, shift)]
        sums = [jnp.sum(r, axis=1, keepdims=True) for r in raised]
        out = None
        for r, value in zip(raised, values):
            term = jnp.dot(r.astype(BF16), value, preferred_element_type=F32)
            out = term if out is None else out + term
        out = out * (1.0 / (sums[0] + sums[1] + sums[2]))
        mixed = jnp.where(lanes == head, out, mixed)
    update = jnp.dot(mixed.astype(BF16), wo_ref[...], preferred_element_type=F32)

    @pl.when(step == 0)
    def _():
        total[...] = start_ref[...] + update

    @pl.when(step > 0)
    def _():
        total[...] += update

    @pl.when(step == pl.num_programs(0) - 1)
    def _():
        after = total[...]
        next_ref[...] = after.astype(BF16)
        mean = jnp.mean(after * after, axis=1, keepdims=True)
        flux_in = (after * lax.rsqrt(mean + 1e-06) * gain_ref[...]).astype(BF16)
        flux = lax.dot_general(
            wf_ref[...], flux_in, (((0,), (1,)), ((), ())), preferred_element_type=F32
        )
        flux_ref[...] = jnp.zeros_like(flux_ref)
        flux_ref[:, 0:rows] = flux.astype(BF16)


def attend(pos, query, kv0, kv1, kv2, w_out, start, gain, w_flux, head_count):
    tokens, width = query.shape
    side = 256
    per = side * head_count // width
    steps = width // side
    flux_count = w_flux.shape[1]
    spec_k = pl.BlockSpec((tokens, side), lambda g: (0, g))
    spec_v = pl.BlockSpec((tokens, side), lambda g: (0, g + steps))
    whole = pl.BlockSpec((tokens, width), lambda g: (0, 0))
    flux_width = up_to(tokens, LANE)
    return pl.pallas_call(
        functools.partial(attend_kernel, per),
        out_shape=(
            jax.ShapeDtypeStruct((tokens, width), BF16),
            jax.ShapeDtypeStruct((flux_count, flux_width), BF16),
        ),
        grid=(steps,),
        in_specs=[SMEM, spec_k, spec_k, spec_v, spec_k, spec_v, spec_k, spec_v]
        + [pl.BlockSpec((side, width), lambda g: (g, 0)), VMEM, VMEM, VMEM],
        out_specs=(whole, pl.BlockSpec((flux_count, flux_width), lambda g: (0, 0))),
        scratch_shapes=[pltpu.VMEM((tokens, width), F32)],
        compiler_params=PARAMS,
        cost_estimate=cost(2e10, 1e7),
        name="attend",
    )(pos, query, kv0, kv0, kv1, kv1, kv2, kv2, w_out, start, gain, w_flux)


def gelu(x):
    inner = x * (0.7978845608028654 + 0.035677408136300125 * (x * x))
    return 0.5 * x * (1.0 + jnp.tanh(inner))


def ocean_kernel(channels, pos_ref, x0, x1, x2, p0, p1, p2, f_ref, w1_ref, w2_ref, out_ref, zbuf, hbuf, state, masks):
    orows, deep, width = x0.shape
    olon = out_ref.shape[2]
    nflux = f_ref.shape[1]
    fwidth = f_ref.shape[2]
    tokens = olon // SPAN
    position, count = pos_ref[0], pos_ref[1]
    odd = position % 2
    high = 3 * deep + 3 * nflux
    hid = w1_ref.shape[0]

    def put_state(row, values):
        zbuf[row, 0:deep] = pltpu.roll(values, 1, 1).astype(BF16)
        zbuf[row, deep : 2 * deep] = values.astype(BF16)
        zbuf[row, 2 * deep : 3 * deep] = pltpu.roll(values, width - 1, 1).astype(BF16)

    blocks = (
        (x0, p0, orows),
        (x1, p1, 2 * orows * (1 - odd)),
        (x2, p2, 2 * orows * odd),
    )
    expand = jnp.where(
        iota((LANE, SPAN * LANE), 0) == iota((LANE, SPAN * LANE), 1) // SPAN, 1.0, 0.0
    ).astype(BF16)
    flane = iota((1, fwidth), 1)
    for x_ref, p_ref, base in blocks:
        block = base // orows
        for i in range(orows):
            row = base + i
            values = x_ref[i].astype(F32)
            put_state(row, values)
            state[row] = values[0:80]
            masks[pl.ds(row, 1)] = values[channels : channels + 1][None]
            weights = (
                p_ref[20 + i : 21 + i, 0:LANE].astype(F32)
                + p_ref[24 + i : 25 + i, 0:LANE].astype(F32)
                + p_ref[28 + i : 29 + i, 0:LANE].astype(F32)
            )
            begin = p_ref[20 + i : 21 + i, 2:3].astype(F32)
            total = None
            for d in (-1, 0, 1):
                coef = jnp.where(begin == d, weights[:, 0:1], 0.0) + jnp.where(
                    begin + 1.0 == d, weights[:, 1:2], 0.0
                )
                term = coef * f_ref[block + 1 + d].astype(F32)
                total = term if total is None else total + term
            ahead = pltpu.roll(total, tokens, 1)
            behind = pltpu.roll(total, fwidth - tokens, 1)
            total = jnp.where(flane == tokens, ahead, total)
            total = jnp.where(flane == fwidth - 1, behind, total)
            total = total.astype(BF16)
            spread = jnp.concatenate(
                [
                    jnp.dot(total[:, at : at + LANE], expand, preferred_element_type=F32)
                    for at in range(0, fwidth, LANE)
                ],
                axis=1,
            )
            at = 3 * deep
            zbuf[row, at : at + nflux] = pltpu.roll(spread, 1, 1).astype(BF16)
            zbuf[row, at + nflux : at + 2 * nflux] = spread.astype(BF16)
            zbuf[row, at + 2 * nflux : at + 3 * nflux] = pltpu.roll(spread, width - 1, 1).astype(BF16)

    def hidden_row(row, zrow, slot):
        taps = zbuf[pl.ds(zrow, 3)].reshape(3 * high, width)
        values = gelu(jnp.dot(w1_ref[...], taps, preferred_element_type=F32))
        place = position * orows + row
        keep = (place >= 0) & (place < count * orows)
        values = values * jnp.where(keep, 1.0, 0.0).astype(F32)
        hbuf[slot, 0:hid] = pltpu.roll(values, 1, 1).astype(BF16)
        hbuf[slot, hid : 2 * hid] = values.astype(BF16)
        hbuf[slot, 2 * hid : 3 * hid] = pltpu.roll(values, width - 1, 1).astype(BF16)

    def pair_update(hrow, srow):
        taps = hbuf[pl.ds(hrow, 4)].reshape(4 * 3 * hid, width)
        both = jnp.dot(w2_ref[...], taps, preferred_element_type=F32)
        for k in range(2):
            state[srow + k] += masks[srow + k] * both[80 * k : 80 * k + 80]

    def first_hidden(j, carry):
        hidden_row(j - 3, j, j)
        return carry

    lax.fori_loop(0, orows + 6, first_hidden, 0)

    def first_state(k, carry):
        pair_update(2 * k, 2 * k + 2)
        for m in range(2):
            put_state(2 * k + 2 + m, jnp.concatenate(
                [state[2 * k + 2 + m], jnp.zeros((deep - 80, width), F32)], axis=0
            ) if deep > 80 else state[2 * k + 2 + m])
        return carry

    lax.fori_loop(0, (orows + 4) // 2, first_state, 0)

    def second_hidden(j, carry):
        hidden_row(j - 1, j + 2, j)
        return carry

    lax.fori_loop(0, orows + 2, second_hidden, 0)
    for k in range(orows // 2):
        pair_update(2 * k, 2 * k + orows)
    for i in range(orows):
        out_ref[i] = state[orows + i][0:channels, 0:olon].astype(BF16)


def ocean(pos, xs, messages, flux_rows, conv_first, conv_second, channels, olon):
    orows, deep, width = xs[0].shape
    hid = conv_first.shape[1]
    nflux = flux_rows.shape[1]
    w1 = conv_first.reshape(3, 3, hid, channels + nflux)
    ws = jnp.pad(w1[..., :channels], ((0, 0), (0, 0), (0, 0), (0, deep - channels)))
    ws = ws.transpose(2, 0, 1, 3).reshape(hid, 3, 3 * deep)
    wf = w1[..., channels:].transpose(2, 0, 1, 3).reshape(hid, 3, 3 * nflux)
    w1 = jnp.concatenate([ws, wf], axis=2).reshape(hid, -1)
    w2 = conv_second.transpose(1, 0, 2).reshape(channels, 9 * hid)
    w2 = jnp.concatenate(
        [
            jnp.pad(w2, ((0, 80 - channels), (0, 3 * hid))),
            jnp.pad(w2, ((0, 80 - channels), (3 * hid, 0))),
        ],
        axis=0,
    )
    high = 3 * deep + 3 * nflux
    return pl.pallas_call(
        functools.partial(ocean_kernel, channels),
        out_shape=jax.ShapeDtypeStruct((orows, channels, olon), BF16),
        in_specs=[SMEM] + [VMEM] * 9,
        out_specs=VMEM,
        scratch_shapes=[
            pltpu.VMEM((3 * orows, high, width), BF16),
            pltpu.VMEM((orows + 6, 3 * hid, width), BF16),
            pltpu.VMEM((3 * orows, 80, width), F32),
            pltpu.VMEM((3 * orows, 1, width), F32),
        ],
        compiler_params=PARAMS,
        cost_estimate=cost(2e10, 1e7),
        name="ocean",
    )(pos, *xs, *messages, flux_rows, w1, w2)


def local(
    atmos,
    ocean_state,
    land_mask,
    w_qkv,
    w_out,
    head_scale,
    gain_attn,
    gain_flux,
    w_flux,
    surf_embed,
    flux_start,
    flux_weight,
    surf_start,
    surf_weight,
    conv_first,
    conv_second,
):
    position = lax.axis_index("lat")
    count = lax.axis_size("lat")
    odd = position % 2
    channels, orows, olon = ocean_state.shape
    width = atmos.shape[1]
    head_count = head_scale.shape[0]
    pos = jnp.stack([position, jnp.int32(count)]).astype(jnp.int32)
    depth = width // head_count
    scale = jnp.broadcast_to(
        (head_scale / jnp.sqrt(jnp.float32(depth)))[:, None], (head_count, depth)
    ).reshape(1, width)

    own = surface_message(pos, ocean_state, surf_start, surf_weight, flux_start, flux_weight)
    partner = swap_in_chip(own)
    far = swap_across(jnp.stack([own, partner]))
    cross, cross2 = far[0], far[1]
    atmos_cross = swap_across(atmos)

    def ordered(middle, here, there):
        low = jnp.where(odd == 1, here, there)
        high = jnp.where(odd == 1, there, here)
        return low, middle, high

    gain_a = gain_attn.reshape(1, width)
    start, query, kv_own = project(
        pos, atmos, ordered(own, partner, cross), surf_embed, gain_a, scale, w_qkv, orows, True
    )
    kv_partner = swap_in_chip(kv_own)
    xs_own = relayout(ocean_state, land_mask)
    xs_partner = swap_in_chip(xs_own)
    xs_cross = swap_across(xs_own)
    (kv_cross,) = project(
        pos, atmos_cross, ordered(cross, own, cross2), surf_embed, gain_a, scale, w_qkv, orows, False
    )
    atmos_next, flux = attend(
        pos, query, kv_own, kv_partner, kv_cross, w_out, start, gain_flux.reshape(1, width), w_flux, head_count
    )
    flux_partner = swap_in_chip(flux)
    flux_far = swap_across(jnp.stack([flux, flux_partner]))
    flux_far2 = swap_in_chip(flux_far)
    even_rows = jnp.stack([flux_far[1], flux_far[0], flux, flux_partner, flux_far2[0]])
    odd_rows = jnp.stack([flux_far2[0], flux_partner, flux, flux_far[0], flux_far[1]])
    flux_rows = jnp.where(odd == 1, odd_rows, even_rows)
    ocean_next = ocean(
        pos,
        (xs_own, xs_partner, xs_cross),
        (own, partner, cross),
        flux_rows,
        conv_first,
        conv_second,
        channels,
        olon,
    )
    return atmos_next, ocean_next.transpose(1, 0, 2)


def solution(mesh):
    in_specs = (
        P(("ens", "lat"), None),
        P(None, ("ens", "lat"), None),
        P("lat", None),
        P(),
        P(),
        P(),
        P(),
        P(),
        P(),
        P(),
        P("lat"),
        P("lat", None),
        P("lat"),
        P("lat", None),
        P(),
        P(),
    )
    out_specs = (P(("ens", "lat"), None), P(None, ("ens", "lat"), None))
    return jax.shard_map(local, mesh=mesh, in_specs=in_specs, out_specs=out_specs, check_vma=False)
```

```python
import functools

import jax
import jax.numpy as jnp
from jax import lax
from jax.experimental import pallas as pl
from jax.experimental.pallas import tpu as pltpu
from jax.sharding import PartitionSpec as P

LEVELS = 19
VARS = 4
SPAN = 4
PSIDE = 1024
WIDE = 256
LANE = 128
F32 = jnp.float32
BF16 = jnp.bfloat16
VMEM = pl.BlockSpec(memory_space=pltpu.VMEM)
SMEM = pl.BlockSpec(memory_space=pltpu.SMEM)


def limit(mebibytes):
    return pltpu.CompilerParams(vmem_limit_bytes=mebibytes * 2**20)


def cost(flops, size):
    return pl.CostEstimate(flops=int(flops), bytes_accessed=int(size), transcendentals=0)


def up_to(value, unit):
    return (value + unit - 1) // unit * unit


def iota(shape, axis):
    return lax.broadcasted_iota(jnp.int32, shape, axis)


def swap_in_chip(block):
    count = lax.axis_size("lat")
    return lax.ppermute(block, "lat", [(i, i ^ 1) for i in range(count)])


def swap_across(block):
    count = lax.axis_size("lat")
    pairs = []
    for i in range(1, count - 1, 2):
        pairs += [(i, i + 1), (i + 1, i)]
    return lax.ppermute(block, "lat", pairs)


def split3(values):
    high = values.astype(BF16)
    rest = values - high.astype(F32)
    middle = rest.astype(BF16)
    low = (rest - middle.astype(F32)).astype(BF16)
    return high, middle, low


def surface_kernel(pos_ref, sstart_ref, fstart_ref, sw_ref, fw_ref, *refs):
    count = fstart_ref.shape[1]
    band = fw_ref.shape[0]
    fields = refs[:VARS]
    out_ref, tile = refs[VARS], refs[VARS + 1]
    orows, olon = fields[0].shape[1:]
    wide = SPAN * LANE
    parts = jnp.concatenate([f[0].astype(F32) for f in fields], axis=0).astype(BF16)
    gather = jnp.where(iota((wide, LANE), 0) // SPAN == iota((wide, LANE), 1), 1.0 / SPAN, 0.0)
    gather = gather.astype(BF16)
    tile[...] = jnp.zeros_like(tile)
    for at in range(0, olon, wide):
        size = min(wide, olon - at)
        tile[0:16, at // SPAN : at // SPAN + LANE] = jnp.dot(
            parts[:, at : at + size], gather[:size], preferred_element_type=F32
        )
    weights = sw_ref.shape[1]
    for index, piece in enumerate(split3(sw_ref[...])):
        tile[16 + index : 17 + index, 0:weights] = piece.astype(F32)
    position = pos_ref[0]
    tile[19:20, 0:1] = (sstart_ref[...] - position * orows).astype(F32)
    for index, piece in enumerate(split3(fw_ref[...])):
        at = 20 + band * index
        tile[at : at + band, 0:count] = piece.astype(F32)
    tile[26:27, 0:count] = (fstart_ref[...] - position).astype(F32)
    out_ref[...] = tile[...].astype(BF16)


def surface_message(pos, ocean_state, surf_start, surf_weight, flux_start, flux_weight):
    channels, orows, olon = ocean_state.shape
    width = up_to(olon // SPAN, LANE)
    specs = [
        pl.BlockSpec((1, orows, olon), functools.partial(lambda v, i: (v * LEVELS, 0, 0), v))
        for v in range(VARS)
    ]
    return pl.pallas_call(
        surface_kernel,
        out_shape=jax.ShapeDtypeStruct((32, width), BF16),
        grid=(1,),
        in_specs=[SMEM, VMEM, VMEM, VMEM, VMEM] + specs,
        out_specs=pl.BlockSpec((32, width), lambda i: (0, 0)),
        scratch_shapes=[pltpu.VMEM((32, width), F32)],
        compiler_params=limit(58),
        cost_estimate=cost(1e12, 1e9),
        name="surface",
    )(
        pos,
        surf_start.reshape(1, -1),
        flux_start.reshape(1, -1),
        surf_weight,
        flux_weight.T,
        *([ocean_state] * VARS),
    )


def relayout_kernel(ocean_ref, mask_ref, after_ref, out_ref, wide, row_ref):
    channels, orows, olon = ocean_ref.shape
    width = out_ref.shape[2]
    wide[...] = ocean_ref[...].astype(F32)
    row_ref[...] = jnp.zeros_like(row_ref)
    pad = width - olon
    lanes = iota((1, width), 1)
    for row in range(orows):
        row_ref[0:channels, 0:olon] = wide[:, row, :]
        row_ref[channels : channels + 1, 0:olon] = mask_ref[row : row + 1, :].astype(F32)
        values = row_ref[...]
        ahead = pltpu.roll(values, olon, 1)
        behind = pltpu.roll(values, pad, 1)
        values = jnp.where((lanes >= olon) & (lanes < olon + SPAN), ahead, values)
        values = jnp.where(lanes >= width - SPAN, behind, values)
        out_ref[row] = values.astype(BF16)


def relayout(ocean_state, land_mask, after):
    channels, orows, olon = ocean_state.shape
    width = up_to(olon + 2 * SPAN, LANE)
    deep = up_to(channels + 1, 16)
    return pl.pallas_call(
        relayout_kernel,
        out_shape=jax.ShapeDtypeStruct((orows, deep, width), BF16),
        in_specs=[VMEM, VMEM, pl.BlockSpec(memory_space=pl.ANY)],
        out_specs=VMEM,
        scratch_shapes=[pltpu.VMEM((channels, orows, olon), F32), pltpu.VMEM((deep, width), F32)],
        compiler_params=limit(16),
        cost_estimate=cost(1e12, 1e9),
        name="relayout",
    )(ocean_state, land_mask, after)


def head_norm(block):
    side = 256
    ones = jnp.where(iota((side, side), 0) // 64 == iota((side, side), 1) // 64, 1.0, 0.0)
    ones = ones.astype(BF16)
    out = []
    for at in range(0, block.shape[1], side):
        part = block[:, at : at + side]
        square = part * part
        high = square.astype(BF16)
        low = (square - high.astype(F32)).astype(BF16)
        total = jnp.dot(high, ones, preferred_element_type=F32)
        total = total + jnp.dot(low, ones, preferred_element_type=F32)
        out.append(part * lax.rsqrt(total * (1.0 / 64) + 1e-06))
    return jnp.concatenate(out, axis=1)


def tokens_start(atmos, embed, sfields, places, params, orows):
    starts = params[19:20, 0:1].astype(F32)
    weights = (
        params[16:17].astype(F32) + params[17:18].astype(F32) + params[18:19].astype(F32)
    )[:, 0:LANE]
    rows = iota((16, LANE), 0) % orows
    lanes = iota((16, LANE), 1)
    total = None
    for block, fields in zip(places, sfields):
        place = rows + block * orows - starts.astype(jnp.int32)
        coef = jnp.sum(jnp.where(lanes == place, weights, 0.0), axis=1, keepdims=True)
        term = coef * fields[0:16].astype(F32)
        total = term if total is None else total + term
    a = split3(total)
    rep = jnp.concatenate(
        [jnp.broadcast_to(embed[v : v + 1], (orows, embed.shape[1])) for v in range(VARS)], axis=0
    )
    b = split3(rep)
    left = jnp.concatenate([a[0], a[0], a[0], a[1], a[1], a[2]], axis=0)
    right = jnp.concatenate([b[0], b[1], b[2], b[0], b[1], b[0]], axis=0)
    added = lax.dot_general(left, right, (((0,), (0,)), ((), ())), preferred_element_type=F32)
    return atmos.astype(F32) + added[: atmos.shape[0]]


def project_kernel(with_query, orows, pos_ref, scale_ref, atmos_ref, m0, m1, m2, embed_ref, gain_ref, w_ref, after_ref, *refs):
    outs = refs
    width, columns = w_ref.shape
    depth = width // scale_ref.shape[0]
    side = min(PSIDE, width)
    toward = 1 - 2 * (pos_ref[0] % 2)
    start = tokens_start(
        atmos_ref[...],
        embed_ref[...],
        (m0[...], m1[...], m2[...]),
        (0, toward, -toward),
        m0[...],
        orows,
    )
    mean = jnp.mean(start * start, axis=1, keepdims=True)
    normed = (start * lax.rsqrt(mean + 1e-06) * gain_ref[...]).astype(BF16)
    if with_query:
        outs[0][...] = start
    for at in range(0 if with_query else width, columns, side):
        block = jnp.dot(normed, w_ref[:, at : at + side], preferred_element_type=F32)
        if at < 2 * width:
            block = head_norm(block)
        if at < width:
            heads = iota((1, side), 1) // depth
            scale = jnp.zeros((1, side), F32)
            for h in range(side // depth):
                scale = jnp.where(heads == h, scale_ref[at // depth + h], scale)
            outs[1][:, at : at + side] = (
                block * (scale / jnp.sqrt(jnp.float32(depth)))
            ).astype(BF16)
        else:
            outs[-1][:, at - width : at - width + side] = block.astype(BF16)


def project(pos, atmos, messages, surf_embed, gain, scale, w_qkv, orows, with_query, after):
    tokens, width = atmos.shape
    out_shape = (jax.ShapeDtypeStruct((tokens, 2 * width), BF16),)
    if with_query:
        out_shape = (
            jax.ShapeDtypeStruct((tokens, width), F32),
            jax.ShapeDtypeStruct((tokens, width), BF16),
        ) + out_shape
    return pl.pallas_call(
        functools.partial(project_kernel, with_query, orows),
        out_shape=out_shape,
        in_specs=[SMEM, SMEM] + [VMEM] * 7 + [pl.BlockSpec(memory_space=pl.ANY)],
        out_specs=(VMEM,) * len(out_shape),
        compiler_params=limit(20),
        cost_estimate=cost(1e12, 1e9),
        name="project",
    )(pos, scale, atmos, *messages, surf_embed, gain, w_qkv, after)


def score_part(query, lanes, per, parts):
    none = jnp.zeros_like(query)
    tops = sums = mixed = None
    for head in range(per):
        mine = jnp.where(lanes == head, query, none)
        scores = [
            lax.dot_general(mine, key, (((1,), (1,)), ((), ())), preferred_element_type=F32)
            for key, _ in parts
        ]
        top = functools.reduce(jnp.maximum, [jnp.max(s, axis=1, keepdims=True) for s in scores])
        raised = [jnp.exp(s - top) for s in scores]
        total = sum(jnp.sum(r, axis=1, keepdims=True) for r in raised)
        out = sum(
            jnp.dot(r.astype(BF16), value, preferred_element_type=F32)
            for r, (_, value) in zip(raised, parts)
        )
        if head == 0:
            shape = out.shape
            tops, sums = jnp.broadcast_to(top, shape), jnp.broadcast_to(total, shape)
            mixed = out
        else:
            tops = jnp.where(lanes == head, top, tops)
            sums = jnp.where(lanes == head, total, sums)
            mixed = jnp.where(lanes == head, out, mixed)
    return tops, sums, mixed


def near_kernel(heads, q_ref, kv0, kv1, top_ref, sum_ref, mix_ref):
    rows, width = q_ref.shape
    per = WIDE * heads // width
    lanes = iota((1, WIDE), 1) // (width // heads)
    for at in range(0, width, WIDE):
        part = slice(at, at + WIDE)
        there = slice(width + at, width + at + WIDE)
        parts = [(kv[:, part], kv[:, there]) for kv in (kv0, kv1)]
        tops, sums, mixed = score_part(q_ref[:, part], lanes, per, parts)
        top_ref[:, part] = tops
        sum_ref[:, part] = sums
        mix_ref[:, part] = mixed


def attend_near(query, kv0, kv1, head_count):
    shape = jax.ShapeDtypeStruct(query.shape, F32)
    return pl.pallas_call(
        functools.partial(near_kernel, head_count),
        out_shape=(shape,) * 3,
        in_specs=[VMEM] * 3,
        out_specs=(VMEM,) * 3,
        compiler_params=limit(16),
        cost_estimate=cost(1, 1),
        name="near",
    )(query, kv0, kv1)


def far_kernel(heads, count, pos_ref, q_ref, kv_ref, top_ref, sum_ref, mix_ref, wo_ref, start_ref, gain_ref, wf_ref, next_ref, flux_ref, total):
    rows, width = q_ref.shape
    per = WIDE * heads // width
    lanes = iota((1, WIDE), 1) // (width // heads)
    position = pos_ref[0]
    exists = ((position > 0) | (position % 2 == 1)) & (
        (position < count - 1) | (position % 2 == 0)
    )
    penalty = jnp.where(exists, 0.0, 1e30).astype(F32)
    for at in range(0, width, WIDE):
        part = slice(at, at + WIDE)
        there = slice(width + at, width + at + WIDE)
        tops, sums, mixed = score_part(
            q_ref[:, part], lanes, per, [(kv_ref[:, part], kv_ref[:, there])]
        )
        tops = tops - penalty
        top = jnp.maximum(tops, top_ref[:, part])
        here, before = jnp.exp(tops - top), jnp.exp(top_ref[:, part] - top)
        mixed = mixed * here + mix_ref[:, part] * before
        mixed = mixed / (sums * here + sum_ref[:, part] * before)
        update = jnp.dot(mixed.astype(BF16), wo_ref[part], preferred_element_type=F32)
        total[...] = (start_ref if at == 0 else total)[...] + update
    after = total[...]
    next_ref[...] = after.astype(BF16)
    mean = jnp.mean(after * after, axis=1, keepdims=True)
    flux_in = (after * lax.rsqrt(mean + 1e-06) * gain_ref[...]).astype(BF16)
    flux = lax.dot_general(
        wf_ref[...], flux_in, (((1,), (1,)), ((), ())), preferred_element_type=F32
    )
    flux_ref[...] = jnp.zeros_like(flux_ref)
    flux_ref[:, 0:rows] = flux.astype(BF16)


def attend_far(pos, query, kv, near, w_out, start, gain, w_flux, head_count, count):
    tokens, width = query.shape
    flux_count = w_flux.shape[0]
    flux_width = up_to(tokens, LANE)
    return pl.pallas_call(
        functools.partial(far_kernel, head_count, count),
        out_shape=(
            jax.ShapeDtypeStruct((tokens, width), BF16),
            jax.ShapeDtypeStruct((flux_count, flux_width), BF16),
        ),
        in_specs=[SMEM] + [VMEM] * 9,
        out_specs=(VMEM, VMEM),
        scratch_shapes=[pltpu.VMEM((tokens, width), F32)],
        compiler_params=limit(20),
        cost_estimate=cost(1e12, 1e9),
        name="far",
    )(pos, query, kv, *near, w_out, start, gain, w_flux)


def gelu(x):
    inner = x * (0.7978845608028654 + 0.035677408136300125 * (x * x))
    return 0.5 * x * (1.0 + jnp.tanh(inner))


def ocean_kernel(channels, count, pos_ref, x0, x1, x2, p0, p1, p2, f0, f1, fx, fy, c1_ref, c2_ref, out_ref, zbuf, hbuf, state, masks, f_ref, w1_ref, w2_ref, w1t, turned):
    orows, deep, width = x0.shape
    olon = out_ref.shape[2]
    nflux = f_ref.shape[1]
    fwidth = f_ref.shape[2]
    tokens = olon // SPAN
    position = pos_ref[0]
    odd = position % 2
    toward = 1 - 2 * odd
    high = 3 * deep + 3 * nflux
    hid = w1_ref.shape[0]

    f_ref[2] = f0[...]
    f_ref[2 + toward] = f1[...]
    f_ref[2 - toward] = fx[0]
    f_ref[2 - 2 * toward] = fx[1]
    f_ref[2 + 2 * toward] = fy[0]

    w1t[...] = jnp.zeros_like(w1t)
    w2_ref[...] = jnp.zeros_like(w2_ref)
    for tap in range(9):
        di, dl = tap // 3, tap % 3
        values = c1_ref[tap].astype(F32)
        at = di * high + dl * deep
        w1t[at : at + channels] = values[:channels]
        at = di * high + 3 * deep + dl * nflux
        w1t[at : at + nflux] = values[channels:]
        for k in range(2):
            at = (tap + 3 * k) * hid
            w2_ref[80 * k : 80 * k + channels, at : at + hid] = c2_ref[tap]
    w1_ref[...] = w1t[...].T.astype(BF16)

    def put_state(row, values):
        zbuf[row, 0:deep] = pltpu.roll(values, 1, 1).astype(BF16)
        zbuf[row, deep : 2 * deep] = values.astype(BF16)
        zbuf[row, 2 * deep : 3 * deep] = pltpu.roll(values, width - 1, 1).astype(BF16)

    blocks = (
        (x0, p0, orows),
        (x1, p1, 2 * orows * (1 - odd)),
        (x2, p2, 2 * orows * odd),
    )
    expand = jnp.where(
        iota((LANE, SPAN * LANE), 0) == iota((LANE, SPAN * LANE), 1) // SPAN, 1.0, 0.0
    ).astype(BF16)
    flane = iota((1, fwidth), 1)
    for x_ref, p_ref, base in blocks:
        block = base // orows
        for i in range(orows):
            row = base + i
            values = x_ref[i].astype(F32)
            put_state(row, values)
            state[row] = values[0:80]
            masks[pl.ds(row, 1)] = values[channels : channels + 1][None]
            first, second = (
                p_ref[20 + b : 21 + b, i : i + 1].astype(F32)
                + p_ref[22 + b : 23 + b, i : i + 1].astype(F32)
                + p_ref[24 + b : 25 + b, i : i + 1].astype(F32)
                for b in range(2)
            )
            begin = p_ref[26:27, i : i + 1].astype(F32)
            total = None
            for d in (-1, 0, 1):
                coef = jnp.where(begin == d, first, 0.0) + jnp.where(
                    begin + 1.0 == d, second, 0.0
                )
                term = coef * f_ref[block + 1 + d].astype(F32)
                total = term if total is None else total + term
            ahead = pltpu.roll(total, tokens, 1)
            behind = pltpu.roll(total, fwidth - tokens, 1)
            total = jnp.where(flane == tokens, ahead, total)
            total = jnp.where(flane == fwidth - 1, behind, total)
            total = total.astype(BF16)
            spread = jnp.concatenate(
                [
                    jnp.dot(total[:, at : at + LANE], expand, preferred_element_type=F32)
                    for at in range(0, fwidth, LANE)
                ],
                axis=1,
            )
            at = 3 * deep
            zbuf[row, at : at + nflux] = pltpu.roll(spread, 1, 1).astype(BF16)
            zbuf[row, at + nflux : at + 2 * nflux] = spread.astype(BF16)
            zbuf[row, at + 2 * nflux : at + 3 * nflux] = pltpu.roll(spread, width - 1, 1).astype(BF16)

    def hidden_row(row, zrow, slot):
        taps = zbuf[pl.ds(zrow, 3)].reshape(3 * high, width)
        values = gelu(jnp.dot(w1_ref[...], taps, preferred_element_type=F32))
        place = position * orows + row
        keep = (place >= 0) & (place < count * orows)
        values = values * jnp.where(keep, 1.0, 0.0).astype(F32)
        hbuf[slot, 0:hid] = pltpu.roll(values, 1, 1).astype(BF16)
        hbuf[slot, hid : 2 * hid] = values.astype(BF16)
        hbuf[slot, 2 * hid : 3 * hid] = pltpu.roll(values, width - 1, 1).astype(BF16)

    def pair_update(hrow, srow):
        taps = hbuf[pl.ds(hrow, 4)].reshape(4 * 3 * hid, width)
        both = jnp.dot(w2_ref[...], taps, preferred_element_type=F32)
        for k in range(2):
            state[srow + k] += masks[srow + k] * both[80 * k : 80 * k + 80]

    def first_hidden(j, carry):
        hidden_row(j - 3, j, j)
        return carry

    lax.fori_loop(0, orows + 6, first_hidden, 0, unroll=True)

    def first_state(k, carry):
        pair_update(2 * k, 2 * k + 2)
        for m in range(2):
            put_state(2 * k + 2 + m, jnp.concatenate(
                [state[2 * k + 2 + m], jnp.zeros((deep - 80, width), F32)], axis=0
            ) if deep > 80 else state[2 * k + 2 + m])
        return carry

    lax.fori_loop(0, (orows + 4) // 2, first_state, 0, unroll=True)

    def second_hidden(j, carry):
        hidden_row(j - 1, j + 2, j)
        return carry

    lax.fori_loop(0, orows + 2, second_hidden, 0, unroll=True)
    for k in range(orows // 2):
        pair_update(2 * k, 2 * k + orows)
    for i in range(orows):
        turned[:, i, :] = state[orows + i][0:channels, 0:olon]
    out_ref[...] = turned[...].astype(BF16)


def ocean(pos, xs, messages, flux, conv_first, conv_second, channels, olon, count):
    orows, deep, width = xs[0].shape
    hid = conv_second.shape[2]
    nflux, fwidth = flux[0].shape
    high = 3 * deep + 3 * nflux
    return pl.pallas_call(
        functools.partial(ocean_kernel, channels, count),
        out_shape=jax.ShapeDtypeStruct((channels, orows, olon), BF16),
        in_specs=[SMEM] + [VMEM] * 12,
        out_specs=VMEM,
        scratch_shapes=[
            pltpu.VMEM((3 * orows, high, width), BF16),
            pltpu.VMEM((orows + 6, 3 * hid, width), BF16),
            pltpu.VMEM((3 * orows, 80, width), F32),
            pltpu.VMEM((3 * orows, 1, width), F32),
            pltpu.VMEM((5, nflux, fwidth), BF16),
            pltpu.VMEM((hid, 3 * high), BF16),
            pltpu.VMEM((160, 12 * hid), BF16),
            pltpu.VMEM((3 * high, hid), F32),
            pltpu.VMEM((channels, orows, olon), F32),
        ],
        compiler_params=limit(44),
        cost_estimate=cost(2e10, 1e7),
        name="ocean",
    )(pos, *xs, *messages, *flux, conv_first, conv_second)


def local(
    atmos,
    ocean_state,
    land_mask,
    w_qkv,
    w_out,
    head_scale,
    gain_attn,
    gain_flux,
    w_flux,
    surf_embed,
    flux_start,
    flux_weight,
    surf_start,
    surf_weight,
    conv_first,
    conv_second,
):
    position = lax.axis_index("lat")
    count = lax.axis_size("lat")
    channels, orows, olon = ocean_state.shape
    width = atmos.shape[1]
    head_count = head_scale.shape[0]
    pos = position.reshape(1).astype(jnp.int32)

    own = surface_message(pos, ocean_state, surf_start, surf_weight, flux_start, flux_weight)
    partner = swap_in_chip(own)
    far = swap_across(jnp.stack([own, partner]))
    cross, cross2 = far[0], far[1]
    atmos_cross = swap_across(atmos)

    gain_a = gain_attn.reshape(1, width)
    start, query, kv_own = project(
        pos, atmos, (own, partner, cross), surf_embed, gain_a, head_scale, w_qkv, orows, True, own
    )
    kv_partner = swap_in_chip(kv_own)
    xs_own = relayout(ocean_state, land_mask, query)
    near = attend_near(query, kv_own, kv_partner, head_count)
    (kv_cross,) = project(
        pos,
        atmos_cross,
        (cross, own, cross2),
        surf_embed,
        gain_a,
        head_scale,
        w_qkv,
        orows,
        False,
        near[0],
    )
    xs_partner = swap_in_chip(xs_own)
    xs_cross = swap_across(xs_own)
    atmos_next, flux = attend_far(
        pos,
        query,
        kv_cross,
        near,
        w_out,
        start,
        gain_flux.reshape(1, width),
        w_flux.T,
        head_count,
        count,
    )
    flux_partner = swap_in_chip(flux)
    flux_far = swap_across(jnp.stack([flux, flux_partner]))
    flux_far2 = swap_in_chip(flux_far)
    ocean_next = ocean(
        pos,
        (xs_own, xs_partner, xs_cross),
        (own, partner, cross),
        (flux, flux_partner, flux_far, flux_far2),
        conv_first.transpose(0, 2, 1),
        conv_second,
        channels,
        olon,
        count,
    )
    return atmos_next, ocean_next


def solution(mesh):
    in_specs = (
        P(("ens", "lat"), None),
        P(None, ("ens", "lat"), None),
        P("lat", None),
        P(),
        P(),
        P(),
        P(),
        P(),
        P(),
        P(),
        P("lat"),
        P("lat", None),
        P("lat"),
        P("lat", None),
        P(),
        P(),
    )
    out_specs = (P(("ens", "lat"), None), P(None, ("ens", "lat"), None))
    return jax.shard_map(local, mesh=mesh, in_specs=in_specs, out_specs=out_specs, check_vma=False)
```

```python
import functools

import jax
import jax.numpy as jnp
from jax import lax
from jax.experimental import pallas as pl
from jax.experimental.pallas import tpu as pltpu
from jax.sharding import PartitionSpec as P

LEVELS = 19
VARS = 4
SPAN = 4
PSIDE = 1024
WIDE = 256
LANE = 128
F32 = jnp.float32
BF16 = jnp.bfloat16
VMEM = pl.BlockSpec(memory_space=pltpu.VMEM)
SMEM = pl.BlockSpec(memory_space=pltpu.SMEM)


def limit(mebibytes):
    return pltpu.CompilerParams(vmem_limit_bytes=mebibytes * 2**20)


def cost(flops, size):
    return pl.CostEstimate(flops=int(flops), bytes_accessed=int(size), transcendentals=0)


def up_to(value, unit):
    return (value + unit - 1) // unit * unit


def iota(shape, axis):
    return lax.broadcasted_iota(jnp.int32, shape, axis)


def swap_in_chip(block):
    count = lax.axis_size("lat")
    return lax.ppermute(block, "lat", [(i, i ^ 1) for i in range(count)])


def swap_across(block):
    count = lax.axis_size("lat")
    pairs = []
    for i in range(1, count - 1, 2):
        pairs += [(i, i + 1), (i + 1, i)]
    return lax.ppermute(block, "lat", pairs)


def split3(values):
    high = values.astype(BF16)
    rest = values - high.astype(F32)
    middle = rest.astype(BF16)
    low = (rest - middle.astype(F32)).astype(BF16)
    return high, middle, low


def surface_kernel(pos_ref, small_ref, ocean_ref, out_ref, tile, *refs):
    fields, sems = refs
    orows, olon = fields.shape[1:]
    copies = [
        pltpu.make_async_copy(ocean_ref.at[v * LEVELS], fields.at[v], sems.at[v])
        for v in range(VARS)
    ]
    for copy in copies:
        copy.start()
    for copy in copies:
        copy.wait()
    wide = SPAN * LANE
    parts = jnp.concatenate([fields[v].astype(F32) for v in range(VARS)], axis=0).astype(BF16)
    gather = jnp.where(iota((wide, LANE), 0) // SPAN == iota((wide, LANE), 1), 1.0 / SPAN, 0.0)
    gather = gather.astype(BF16)
    tile[...] = jnp.zeros_like(tile)
    for at in range(0, olon, wide):
        size = min(wide, olon - at)
        tile[0:16, at // SPAN : at // SPAN + LANE] = jnp.dot(
            parts[:, at : at + size], gather[:size], preferred_element_type=F32
        )
    lanes = small_ref.shape[1]
    weights = lanes - 1 - orows - 2 * orows
    small = small_ref[...]
    for index, piece in enumerate(split3(small[:, 0:weights])):
        tile[16 + index : 17 + index, 0:weights] = piece.astype(F32)
    position = pos_ref[0].astype(F32)
    for band in range(2):
        at = weights + band * orows
        for index, piece in enumerate(split3(small[:, at : at + orows])):
            row = 20 + 2 * index + band
            tile[row : row + 1, 0:orows] = piece.astype(F32)
    at = weights + 2 * orows
    tile[26:27, 0:orows] = small[:, at : at + orows] - position
    tile[19:20, 0:1] = small[:, at + orows : lanes] - position * orows
    tile[27:28, 0:LANE] = jnp.ones((1, LANE), F32)
    out_ref[...] = tile[...].astype(BF16)


def surface_message(pos, ocean_state, surf_start, surf_weight, flux_start, flux_weight):
    channels, orows, olon = ocean_state.shape
    width = up_to(olon // SPAN, LANE)
    small = jnp.concatenate(
        [
            surf_weight.reshape(-1),
            flux_weight.T.reshape(-1),
            flux_start.astype(F32),
            surf_start.astype(F32),
        ]
    ).reshape(1, -1)
    return pl.pallas_call(
        surface_kernel,
        out_shape=jax.ShapeDtypeStruct((32, width), BF16),
        in_specs=[SMEM, VMEM, pl.BlockSpec(memory_space=pl.ANY)],
        out_specs=VMEM,
        scratch_shapes=[
            pltpu.VMEM((32, width), F32),
            pltpu.VMEM((VARS, orows, olon), BF16),
            pltpu.SemaphoreType.DMA((VARS,)),
        ],
        compiler_params=limit(8),
        cost_estimate=cost(1e12, 1e9),
        name="surface",
    )(pos, small, ocean_state)


def relayout_kernel(ocean_ref, mask_ref, after_ref, out_ref, wide, row_ref):
    channels, orows, olon = ocean_ref.shape
    width = out_ref.shape[2]
    wide[...] = ocean_ref[...].astype(F32)
    row_ref[...] = jnp.zeros_like(row_ref)
    pad = width - olon
    lanes = iota((1, width), 1)
    for row in range(orows):
        row_ref[0:channels, 0:olon] = wide[:, row, :]
        row_ref[channels : channels + 1, 0:olon] = mask_ref[row : row + 1, :].astype(F32)
        values = row_ref[...]
        ahead = pltpu.roll(values, olon, 1)
        behind = pltpu.roll(values, pad, 1)
        values = jnp.where((lanes >= olon) & (lanes < olon + SPAN), ahead, values)
        values = jnp.where(lanes >= width - SPAN, behind, values)
        out_ref[row] = values.astype(BF16)


def relayout(ocean_state, land_mask, after):
    channels, orows, olon = ocean_state.shape
    width = up_to(olon + 2 * SPAN, LANE)
    deep = up_to(channels + 1, 16)
    return pl.pallas_call(
        relayout_kernel,
        out_shape=jax.ShapeDtypeStruct((orows, deep, width), BF16),
        in_specs=[VMEM, VMEM, pl.BlockSpec(memory_space=pl.ANY)],
        out_specs=VMEM,
        scratch_shapes=[pltpu.VMEM((channels, orows, olon), F32), pltpu.VMEM((deep, width), F32)],
        compiler_params=limit(16),
        cost_estimate=cost(1e12, 1e9),
        name="relayout",
    )(ocean_state, land_mask, after)


def head_norm(block):
    side = 256
    ones = jnp.where(iota((side, side), 0) // 64 == iota((side, side), 1) // 64, 1.0, 0.0)
    ones = ones.astype(BF16)
    out = []
    for at in range(0, block.shape[1], side):
        part = block[:, at : at + side]
        square = part * part
        high = square.astype(BF16)
        low = (square - high.astype(F32)).astype(BF16)
        total = jnp.dot(high, ones, preferred_element_type=F32)
        total = total + jnp.dot(low, ones, preferred_element_type=F32)
        out.append(part * lax.rsqrt(total * (1.0 / 64) + 1e-06))
    return jnp.concatenate(out, axis=1)


def tokens_start(atmos, embed, sfields, places, params, orows):
    starts = params[19:20, 0:1].astype(F32)
    weights = (
        params[16:17].astype(F32) + params[17:18].astype(F32) + params[18:19].astype(F32)
    )[:, 0:LANE]
    rows = iota((16, LANE), 0) % orows
    lanes = iota((16, LANE), 1)
    total = None
    for block, fields in zip(places, sfields):
        place = rows + block * orows - starts.astype(jnp.int32)
        coef = jnp.sum(jnp.where(lanes == place, weights, 0.0), axis=1, keepdims=True)
        term = coef * fields[0:16].astype(F32)
        total = term if total is None else total + term
    a = split3(total)
    rep = jnp.concatenate(
        [jnp.broadcast_to(embed[v : v + 1], (orows, embed.shape[1])) for v in range(VARS)], axis=0
    )
    b = split3(rep)
    left = jnp.concatenate([a[0], a[0], a[0], a[1], a[1], a[2]], axis=0)
    right = jnp.concatenate([b[0], b[1], b[2], b[0], b[1], b[0]], axis=0)
    added = lax.dot_general(left, right, (((0,), (0,)), ((), ())), preferred_element_type=F32)
    return atmos.astype(F32) + added[: atmos.shape[0]]


def project_kernel(with_query, orows, pos_ref, scale_ref, atmos_ref, m0, m1, m2, embed_ref, gain_ref, w_ref, after_ref, *refs):
    outs = refs
    width, columns = w_ref.shape
    depth = width // scale_ref.shape[0]
    side = min(PSIDE, width)
    toward = 1 - 2 * (pos_ref[0] % 2)
    start = tokens_start(
        atmos_ref[...],
        embed_ref[...],
        (m0[...], m1[...], m2[...]),
        (0, toward, -toward),
        m0[...],
        orows,
    )
    mean = jnp.mean(start * start, axis=1, keepdims=True)
    normed = (start * lax.rsqrt(mean + 1e-06) * gain_ref[...]).astype(BF16)
    if with_query:
        outs[0][...] = start
    for at in range(0 if with_query else width, columns, side):
        block = jnp.dot(normed, w_ref[:, at : at + side], preferred_element_type=F32)
        if at < 2 * width:
            block = head_norm(block)
        if at < width:
            heads = iota((1, side), 1) // depth
            scale = jnp.zeros((1, side), F32)
            for h in range(side // depth):
                scale = jnp.where(heads == h, scale_ref[at // depth + h], scale)
            outs[1][:, at : at + side] = (
                block * (scale / jnp.sqrt(jnp.float32(depth)))
            ).astype(BF16)
        else:
            outs[-1][:, at - width : at - width + side] = block.astype(BF16)


def project(pos, atmos, messages, surf_embed, gain, scale, w_qkv, orows, with_query, after):
    tokens, width = atmos.shape
    out_shape = (jax.ShapeDtypeStruct((tokens, 2 * width), BF16),)
    if with_query:
        out_shape = (
            jax.ShapeDtypeStruct((tokens, width), F32),
            jax.ShapeDtypeStruct((tokens, width), BF16),
        ) + out_shape
    return pl.pallas_call(
        functools.partial(project_kernel, with_query, orows),
        out_shape=out_shape,
        in_specs=[SMEM, SMEM] + [VMEM] * 7 + [pl.BlockSpec(memory_space=pl.ANY)],
        out_specs=(VMEM,) * len(out_shape),
        compiler_params=limit(20),
        cost_estimate=cost(1e12, 1e9),
        name="project",
    )(pos, scale, atmos, *messages, surf_embed, gain, w_qkv, after)


def score_part(query, lanes, per, parts):
    none = jnp.zeros_like(query)
    tops = sums = mixed = None
    for head in range(per):
        mine = jnp.where(lanes == head, query, none)
        scores = [
            lax.dot_general(mine, key, (((1,), (1,)), ((), ())), preferred_element_type=F32)
            for key, _ in parts
        ]
        top = functools.reduce(jnp.maximum, [jnp.max(s, axis=1, keepdims=True) for s in scores])
        raised = [jnp.exp(s - top) for s in scores]
        total = sum(jnp.sum(r, axis=1, keepdims=True) for r in raised)
        out = sum(
            jnp.dot(r.astype(BF16), value, preferred_element_type=F32)
            for r, (_, value) in zip(raised, parts)
        )
        if head == 0:
            shape = out.shape
            tops, sums = jnp.broadcast_to(top, shape), jnp.broadcast_to(total, shape)
            mixed = out
        else:
            tops = jnp.where(lanes == head, top, tops)
            sums = jnp.where(lanes == head, total, sums)
            mixed = jnp.where(lanes == head, out, mixed)
    return tops, sums, mixed


def near_kernel(heads, q_ref, kv0, kv1, top_ref, sum_ref, mix_ref):
    rows, width = q_ref.shape
    per = WIDE * heads // width
    lanes = iota((1, WIDE), 1) // (width // heads)

    def group(g, carry):
        part = pl.ds(pl.multiple_of(g * WIDE, WIDE), WIDE)
        there = pl.ds(pl.multiple_of(width + g * WIDE, WIDE), WIDE)
        parts = [(kv[:, part], kv[:, there]) for kv in (kv0, kv1)]
        tops, sums, mixed = score_part(q_ref[:, part], lanes, per, parts)
        top_ref[:, part] = tops
        sum_ref[:, part] = sums
        mix_ref[:, part] = mixed
        return carry

    lax.fori_loop(0, width // WIDE, group, 0)


def attend_near(query, kv0, kv1, head_count):
    shape = jax.ShapeDtypeStruct(query.shape, F32)
    return pl.pallas_call(
        functools.partial(near_kernel, head_count),
        out_shape=(shape,) * 3,
        in_specs=[VMEM] * 3,
        out_specs=(VMEM,) * 3,
        compiler_params=limit(16),
        cost_estimate=cost(1, 1),
        name="near",
    )(query, kv0, kv1)


def far_kernel(heads, message_ref, q_ref, kv_ref, top_ref, sum_ref, mix_ref, wo_ref, start_ref, gain_ref, wf_ref, next_ref, flux_ref, total):
    rows, width = q_ref.shape
    per = WIDE * heads // width
    lanes = iota((1, WIDE), 1) // (width // heads)
    penalty = jnp.where(message_ref[27:28, 0:1].astype(F32) > 0.5, 0.0, 1e30)
    total[...] = start_ref[...]

    def group(g, carry):
        part = pl.ds(pl.multiple_of(g * WIDE, WIDE), WIDE)
        there = pl.ds(pl.multiple_of(width + g * WIDE, WIDE), WIDE)
        tops, sums, mixed = score_part(
            q_ref[:, part], lanes, per, [(kv_ref[:, part], kv_ref[:, there])]
        )
        tops = tops - penalty
        top = jnp.maximum(tops, top_ref[:, part])
        here, before = jnp.exp(tops - top), jnp.exp(top_ref[:, part] - top)
        mixed = mixed * here + mix_ref[:, part] * before
        mixed = mixed / (sums * here + sum_ref[:, part] * before)
        total[...] += jnp.dot(mixed.astype(BF16), wo_ref[part], preferred_element_type=F32)
        return carry

    lax.fori_loop(0, width // WIDE, group, 0)
    after = total[...]
    next_ref[...] = after.astype(BF16)
    mean = jnp.mean(after * after, axis=1, keepdims=True)
    flux_in = (after * lax.rsqrt(mean + 1e-06) * gain_ref[...]).astype(BF16)
    flux = lax.dot_general(
        wf_ref[...], flux_in, (((1,), (1,)), ((), ())), preferred_element_type=F32
    )
    flux_ref[...] = jnp.zeros_like(flux_ref)
    flux_ref[:, 0:rows] = flux.astype(BF16)


def attend_far(message, query, kv, near, w_out, start, gain, w_flux, head_count):
    tokens, width = query.shape
    flux_count = w_flux.shape[0]
    flux_width = up_to(tokens, LANE)
    return pl.pallas_call(
        functools.partial(far_kernel, head_count),
        out_shape=(
            jax.ShapeDtypeStruct((tokens, width), BF16),
            jax.ShapeDtypeStruct((flux_count, flux_width), BF16),
        ),
        in_specs=[VMEM] * 10,
        out_specs=(VMEM, VMEM),
        scratch_shapes=[pltpu.VMEM((tokens, width), F32)],
        compiler_params=limit(20),
        cost_estimate=cost(1e12, 1e9),
        name="far",
    )(message, query, kv, *near, w_out, start, gain, w_flux)


def gate_kernel(value_ref, after_ref, out_ref):
    pass


def gate(value, after):
    anywhere = pl.BlockSpec(memory_space=pl.ANY)
    return pl.pallas_call(
        gate_kernel,
        out_shape=jax.ShapeDtypeStruct(value.shape, value.dtype),
        in_specs=[anywhere, anywhere],
        out_specs=anywhere,
        input_output_aliases={0: 0},
        compiler_params=limit(1),
        cost_estimate=cost(1, 1),
        name="gate",
    )(value, after)


def gelu(x):
    inner = x * (0.7978845608028654 + 0.035677408136300125 * (x * x))
    return 0.5 * x * (1.0 + jnp.tanh(inner))


def ocean_kernel(channels, count, pos_ref, x0, x1, x2, p0, p1, p2, f0, f1, fx, fy, c1_ref, c2_ref, next_ref, out_ref, next_hbm, zbuf, hbuf, state, masks, f_ref, w1_ref, w2_ref, w1t, turned, sem):
    copy = pltpu.make_async_copy(next_ref, next_hbm, sem)
    copy.start()
    orows, deep, width = x0.shape
    olon = out_ref.shape[2]
    nflux = f_ref.shape[1]
    fwidth = f_ref.shape[2]
    tokens = olon // SPAN
    position = pos_ref[0]
    odd = position % 2
    toward = 1 - 2 * odd
    high = 3 * deep + 3 * nflux
    hid = w1_ref.shape[0]

    f_ref[2] = f0[...]
    f_ref[2 + toward] = f1[...]
    f_ref[2 - toward] = fx[0]
    f_ref[2 - 2 * toward] = fx[1]
    f_ref[2 + 2 * toward] = fy[0]

    w1t[...] = jnp.zeros_like(w1t)
    w2_ref[...] = jnp.zeros_like(w2_ref)
    for tap in range(9):
        di, dl = tap // 3, tap % 3
        values = c1_ref[tap].astype(F32)
        at = di * high + dl * deep
        w1t[at : at + channels] = values[:channels]
        at = di * high + 3 * deep + dl * nflux
        w1t[at : at + nflux] = values[channels:]
        for k in range(2):
            at = (tap + 3 * k) * hid
            w2_ref[80 * k : 80 * k + channels, at : at + hid] = c2_ref[tap]
    w1_ref[...] = w1t[...].T.astype(BF16)

    def put_state(row, values):
        zbuf[row, 0:deep] = pltpu.roll(values, 1, 1).astype(BF16)
        zbuf[row, deep : 2 * deep] = values.astype(BF16)
        zbuf[row, 2 * deep : 3 * deep] = pltpu.roll(values, width - 1, 1).astype(BF16)

    blocks = (
        (x0, p0, orows),
        (x1, p1, 2 * orows * (1 - odd)),
        (x2, p2, 2 * orows * odd),
    )
    expand = jnp.where(
        iota((LANE, SPAN * LANE), 0) == iota((LANE, SPAN * LANE), 1) // SPAN, 1.0, 0.0
    ).astype(BF16)
    flane = iota((1, fwidth), 1)
    for x_ref, p_ref, base in blocks:
        block = base // orows
        for i in range(orows):
            row = base + i
            values = x_ref[i].astype(F32)
            put_state(row, values)
            state[row] = values[0:80]
            masks[pl.ds(row, 1)] = values[channels : channels + 1][None]
            first, second = (
                p_ref[20 + b : 21 + b, i : i + 1].astype(F32)
                + p_ref[22 + b : 23 + b, i : i + 1].astype(F32)
                + p_ref[24 + b : 25 + b, i : i + 1].astype(F32)
                for b in range(2)
            )
            begin = p_ref[26:27, i : i + 1].astype(F32)
            total = None
            for d in (-1, 0, 1):
                coef = jnp.where(begin == d, first, 0.0) + jnp.where(
                    begin + 1.0 == d, second, 0.0
                )
                term = coef * f_ref[block + 1 + d].astype(F32)
                total = term if total is None else total + term
            ahead = pltpu.roll(total, tokens, 1)
            behind = pltpu.roll(total, fwidth - tokens, 1)
            total = jnp.where(flane == tokens, ahead, total)
            total = jnp.where(flane == fwidth - 1, behind, total)
            total = total.astype(BF16)
            spread = jnp.concatenate(
                [
                    jnp.dot(total[:, at : at + LANE], expand, preferred_element_type=F32)
                    for at in range(0, fwidth, LANE)
                ],
                axis=1,
            )
            at = 3 * deep
            zbuf[row, at : at + nflux] = pltpu.roll(spread, 1, 1).astype(BF16)
            zbuf[row, at + nflux : at + 2 * nflux] = spread.astype(BF16)
            zbuf[row, at + 2 * nflux : at + 3 * nflux] = pltpu.roll(spread, width - 1, 1).astype(BF16)

    def hidden_row(row, zrow, slot):
        taps = zbuf[pl.ds(zrow, 3)].reshape(3 * high, width)
        values = gelu(jnp.dot(w1_ref[...], taps, preferred_element_type=F32))
        place = position * orows + row
        keep = (place >= 0) & (place < count * orows)
        values = values * jnp.where(keep, 1.0, 0.0).astype(F32)
        hbuf[slot, 0:hid] = pltpu.roll(values, 1, 1).astype(BF16)
        hbuf[slot, hid : 2 * hid] = values.astype(BF16)
        hbuf[slot, 2 * hid : 3 * hid] = pltpu.roll(values, width - 1, 1).astype(BF16)

    def pair_update(hrow, srow):
        taps = hbuf[pl.ds(hrow, 4)].reshape(4 * 3 * hid, width)
        both = jnp.dot(w2_ref[...], taps, preferred_element_type=F32)
        for k in range(2):
            state[srow + k] += masks[srow + k] * both[80 * k : 80 * k + 80]

    def first_hidden(j, carry):
        hidden_row(j - 3, j, j)
        return carry

    lax.fori_loop(0, orows + 6, first_hidden, 0, unroll=True)

    def first_state(k, carry):
        pair_update(2 * k, 2 * k + 2)
        for m in range(2):
            put_state(2 * k + 2 + m, jnp.concatenate(
                [state[2 * k + 2 + m], jnp.zeros((deep - 80, width), F32)], axis=0
            ) if deep > 80 else state[2 * k + 2 + m])
        return carry

    lax.fori_loop(0, (orows + 4) // 2, first_state, 0, unroll=True)

    def second_hidden(j, carry):
        hidden_row(j - 1, j + 2, j)
        return carry

    lax.fori_loop(0, orows + 2, second_hidden, 0, unroll=True)
    for k in range(orows // 2):
        pair_update(2 * k, 2 * k + orows)
    for i in range(orows):
        turned[:, i, :] = state[orows + i][0:channels, 0:olon]
    out_ref[...] = turned[...].astype(BF16)
    copy.wait()


def ocean(pos, xs, messages, flux, conv_first, conv_second, tokens, channels, olon, count):
    orows, deep, width = xs[0].shape
    hid = conv_second.shape[2]
    nflux, fwidth = flux[0].shape
    high = 3 * deep + 3 * nflux
    return pl.pallas_call(
        functools.partial(ocean_kernel, channels, count),
        out_shape=(
            jax.ShapeDtypeStruct((channels, orows, olon), BF16),
            jax.ShapeDtypeStruct(tokens.shape, tokens.dtype),
        ),
        in_specs=[SMEM] + [VMEM] * 13,
        out_specs=(VMEM, pl.BlockSpec(memory_space=pltpu.HBM)),
        scratch_shapes=[
            pltpu.VMEM((3 * orows, high, width), BF16),
            pltpu.VMEM((orows + 6, 3 * hid, width), BF16),
            pltpu.VMEM((3 * orows, 80, width), F32),
            pltpu.VMEM((3 * orows, 1, width), F32),
            pltpu.VMEM((5, nflux, fwidth), BF16),
            pltpu.VMEM((hid, 3 * high), BF16),
            pltpu.VMEM((160, 12 * hid), BF16),
            pltpu.VMEM((3 * high, hid), F32),
            pltpu.VMEM((channels, orows, olon), F32),
            pltpu.SemaphoreType.DMA,
        ],
        compiler_params=limit(44),
        cost_estimate=cost(2e10, 1e7),
        name="ocean",
    )(pos, *xs, *messages, *flux, conv_first, conv_second, tokens)


def local(
    atmos,
    ocean_state,
    land_mask,
    w_qkv,
    w_out,
    head_scale,
    gain_attn,
    gain_flux,
    w_flux,
    surf_embed,
    flux_start,
    flux_weight,
    surf_start,
    surf_weight,
    conv_first,
    conv_second,
):
    position = lax.axis_index("lat")
    count = lax.axis_size("lat")
    channels, orows, olon = ocean_state.shape
    width = atmos.shape[1]
    head_count = head_scale.shape[0]
    pos = position.reshape(1).astype(jnp.int32)

    own = surface_message(pos, ocean_state, surf_start, surf_weight, flux_start, flux_weight)
    partner = swap_in_chip(own)
    far = swap_across(jnp.stack([own, partner]))
    cross, cross2 = far[0], far[1]
    atmos_cross = swap_across(atmos)

    gain_a = gain_attn.reshape(1, width)
    start, query, kv_own = project(
        pos, atmos, (own, partner, cross), surf_embed, gain_a, head_scale, w_qkv, orows, True, own
    )
    kv_partner = swap_in_chip(kv_own)
    xs_own = relayout(ocean_state, land_mask, query)
    near = attend_near(query, kv_own, kv_partner, head_count)
    (kv_cross,) = project(
        pos,
        atmos_cross,
        (cross, own, cross2),
        surf_embed,
        gain_a,
        head_scale,
        w_qkv,
        orows,
        False,
        near[0],
    )
    xs_own = gate(xs_own, query)
    xs_partner = swap_in_chip(xs_own)
    xs_cross = swap_across(xs_own)
    atmos_next, flux = attend_far(
        cross,
        query,
        kv_cross,
        near,
        w_out,
        start,
        gain_flux.reshape(1, width),
        w_flux.T,
        head_count,
    )
    flux_partner = swap_in_chip(flux)
    flux_far = swap_across(jnp.stack([flux, flux_partner]))
    flux_far2 = swap_in_chip(flux_far)
    ocean_next, atmos_next = ocean(
        pos,
        (xs_own, xs_partner, xs_cross),
        (own, partner, cross),
        (flux, flux_partner, flux_far, flux_far2),
        conv_first.transpose(0, 2, 1),
        conv_second,
        atmos_next,
        channels,
        olon,
        count,
    )
    return atmos_next, ocean_next


def solution(mesh):
    in_specs = (
        P(("ens", "lat"), None),
        P(None, ("ens", "lat"), None),
        P("lat", None),
        P(),
        P(),
        P(),
        P(),
        P(),
        P(),
        P(),
        P("lat"),
        P("lat", None),
        P("lat"),
        P("lat", None),
        P(),
        P(),
    )
    out_specs = (P(("ens", "lat"), None), P(None, ("ens", "lat"), None))
    return jax.shard_map(local, mesh=mesh, in_specs=in_specs, out_specs=out_specs, check_vma=False)
```

```python
import functools

import jax
import jax.numpy as jnp
from jax import lax
from jax.experimental import pallas as pl
from jax.experimental.pallas import tpu as pltpu
from jax.sharding import PartitionSpec as P

LEVELS = 19
VARS = 4
SPAN = 4
PSIDE = 1024
WIDE = 256
LANE = 128
F32 = jnp.float32
BF16 = jnp.bfloat16
VMEM = pl.BlockSpec(memory_space=pltpu.VMEM)
SMEM = pl.BlockSpec(memory_space=pltpu.SMEM)


def limit(mebibytes):
    return pltpu.CompilerParams(vmem_limit_bytes=mebibytes * 2**20)


def cost(flops, size):
    return pl.CostEstimate(flops=int(flops), bytes_accessed=int(size), transcendentals=0)


def up_to(value, unit):
    return (value + unit - 1) // unit * unit


def iota(shape, axis):
    return lax.broadcasted_iota(jnp.int32, shape, axis)


def swap_in_chip(block):
    count = lax.axis_size("lat")
    return lax.ppermute(block, "lat", [(i, i ^ 1) for i in range(count)])


def swap_across(block):
    count = lax.axis_size("lat")
    pairs = []
    for i in range(1, count - 1, 2):
        pairs += [(i, i + 1), (i + 1, i)]
    return lax.ppermute(block, "lat", pairs)


def split3(values):
    high = values.astype(BF16)
    rest = values - high.astype(F32)
    middle = rest.astype(BF16)
    low = (rest - middle.astype(F32)).astype(BF16)
    return high, middle, low


def surface_kernel(pos_ref, small_ref, ocean_ref, out_ref, tile, *refs):
    fields, sems = refs
    orows, olon = fields.shape[1:]
    copies = [
        pltpu.make_async_copy(ocean_ref.at[v * LEVELS], fields.at[v], sems.at[v])
        for v in range(VARS)
    ]
    for copy in copies:
        copy.start()
    for copy in copies:
        copy.wait()
    wide = SPAN * LANE
    parts = jnp.concatenate([fields[v].astype(F32) for v in range(VARS)], axis=0).astype(BF16)
    gather = jnp.where(iota((wide, LANE), 0) // SPAN == iota((wide, LANE), 1), 1.0 / SPAN, 0.0)
    gather = gather.astype(BF16)
    tile[...] = jnp.zeros_like(tile)
    for at in range(0, olon, wide):
        size = min(wide, olon - at)
        tile[0:16, at // SPAN : at // SPAN + LANE] = jnp.dot(
            parts[:, at : at + size], gather[:size], preferred_element_type=F32
        )
    lanes = small_ref.shape[1]
    weights = lanes - 1 - orows - 2 * orows
    small = small_ref[...]
    for index, piece in enumerate(split3(small[:, 0:weights])):
        tile[16 + index : 17 + index, 0:weights] = piece.astype(F32)
    position = pos_ref[0].astype(F32)
    for band in range(2):
        at = weights + band * orows
        for index, piece in enumerate(split3(small[:, at : at + orows])):
            row = 20 + 2 * index + band
            tile[row : row + 1, 0:orows] = piece.astype(F32)
    at = weights + 2 * orows
    tile[26:27, 0:orows] = small[:, at : at + orows] - position
    tile[19:20, 0:1] = small[:, at + orows : lanes] - position * orows
    tile[27:28, 0:LANE] = jnp.ones((1, LANE), F32)
    out_ref[...] = tile[...].astype(BF16)


def surface_message(pos, ocean_state, surf_start, surf_weight, flux_start, flux_weight):
    channels, orows, olon = ocean_state.shape
    width = up_to(olon // SPAN, LANE)
    bands = flux_weight.T
    pieces = [surf_weight, bands[0:1], bands[1:2]]
    pieces += [flux_start.astype(F32).reshape(1, -1), surf_start.astype(F32).reshape(1, -1)]
    lanes = sum(piece.shape[1] for piece in pieces)
    small, at = None, 0
    for piece in pieces:
        size = piece.shape[1]
        padded = jnp.pad(piece, ((0, 0), (at, lanes - at - size)))
        small = padded if small is None else small + padded
        at += size
    return pl.pallas_call(
        surface_kernel,
        out_shape=jax.ShapeDtypeStruct((32, width), BF16),
        in_specs=[SMEM, VMEM, pl.BlockSpec(memory_space=pl.ANY)],
        out_specs=VMEM,
        scratch_shapes=[
            pltpu.VMEM((32, width), F32),
            pltpu.VMEM((VARS, orows, olon), BF16),
            pltpu.SemaphoreType.DMA((VARS,)),
        ],
        compiler_params=limit(8),
        cost_estimate=cost(1e12, 1e9),
        name="surface",
    )(pos, small, ocean_state)


def relayout_kernel(ocean_ref, mask_ref, after_ref, out_ref, wide, row_ref):
    channels, orows, olon = ocean_ref.shape
    width = out_ref.shape[2]
    wide[...] = ocean_ref[...].astype(F32)
    row_ref[...] = jnp.zeros_like(row_ref)
    pad = width - olon
    lanes = iota((1, width), 1)
    for row in range(orows):
        row_ref[0:channels, 0:olon] = wide[:, row, :]
        row_ref[channels : channels + 1, 0:olon] = mask_ref[row : row + 1, :].astype(F32)
        values = row_ref[...]
        ahead = pltpu.roll(values, olon, 1)
        behind = pltpu.roll(values, pad, 1)
        values = jnp.where((lanes >= olon) & (lanes < olon + SPAN), ahead, values)
        values = jnp.where(lanes >= width - SPAN, behind, values)
        out_ref[row] = values.astype(BF16)


def relayout(ocean_state, land_mask, after):
    channels, orows, olon = ocean_state.shape
    width = up_to(olon + 2 * SPAN, LANE)
    deep = up_to(channels + 1, 16)
    return pl.pallas_call(
        relayout_kernel,
        out_shape=jax.ShapeDtypeStruct((orows, deep, width), BF16),
        in_specs=[VMEM, VMEM, pl.BlockSpec(memory_space=pl.ANY)],
        out_specs=VMEM,
        scratch_shapes=[pltpu.VMEM((channels, orows, olon), F32), pltpu.VMEM((deep, width), F32)],
        compiler_params=limit(16),
        cost_estimate=cost(1e12, 1e9),
        name="relayout",
    )(ocean_state, land_mask, after)


def head_norm(block):
    side = 256
    ones = jnp.where(iota((side, side), 0) // 64 == iota((side, side), 1) // 64, 1.0, 0.0)
    ones = ones.astype(BF16)
    out = []
    for at in range(0, block.shape[1], side):
        part = block[:, at : at + side]
        square = part * part
        high = square.astype(BF16)
        low = (square - high.astype(F32)).astype(BF16)
        total = jnp.dot(high, ones, preferred_element_type=F32)
        total = total + jnp.dot(low, ones, preferred_element_type=F32)
        out.append(part * lax.rsqrt(total * (1.0 / 64) + 1e-06))
    return jnp.concatenate(out, axis=1)


def tokens_start(atmos, embed, sfields, places, params, orows):
    starts = params[19:20, 0:1].astype(F32)
    weights = (
        params[16:17].astype(F32) + params[17:18].astype(F32) + params[18:19].astype(F32)
    )[:, 0:LANE]
    rows = iota((16, LANE), 0) % orows
    lanes = iota((16, LANE), 1)
    total = None
    for block, fields in zip(places, sfields):
        place = rows + block * orows - starts.astype(jnp.int32)
        coef = jnp.sum(jnp.where(lanes == place, weights, 0.0), axis=1, keepdims=True)
        term = coef * fields[0:16].astype(F32)
        total = term if total is None else total + term
    a = split3(total)
    rep = jnp.concatenate(
        [jnp.broadcast_to(embed[v : v + 1], (orows, embed.shape[1])) for v in range(VARS)], axis=0
    )
    b = split3(rep)
    left = jnp.concatenate([a[0], a[0], a[0], a[1], a[1], a[2]], axis=0)
    right = jnp.concatenate([b[0], b[1], b[2], b[0], b[1], b[0]], axis=0)
    added = lax.dot_general(left, right, (((0,), (0,)), ((), ())), preferred_element_type=F32)
    return atmos.astype(F32) + added[: atmos.shape[0]]


def project_kernel(with_query, orows, pos_ref, scale_ref, atmos_ref, m0, m1, m2, embed_ref, gain_ref, w_ref, after_ref, *refs):
    outs = refs
    width, columns = w_ref.shape
    depth = width // scale_ref.shape[0]
    side = min(PSIDE, width)
    toward = 1 - 2 * (pos_ref[0] % 2)
    start = tokens_start(
        atmos_ref[...],
        embed_ref[...],
        (m0[...], m1[...], m2[...]),
        (0, toward, -toward),
        m0[...],
        orows,
    )
    mean = jnp.mean(start * start, axis=1, keepdims=True)
    normed = (start * lax.rsqrt(mean + 1e-06) * gain_ref[...]).astype(BF16)
    if with_query:
        outs[0][...] = start
    for at in range(0 if with_query else width, columns, side):
        block = jnp.dot(normed, w_ref[:, at : at + side], preferred_element_type=F32)
        if at < 2 * width:
            block = head_norm(block)
        if at < width:
            heads = iota((1, side), 1) // depth
            scale = jnp.zeros((1, side), F32)
            for h in range(side // depth):
                scale = jnp.where(heads == h, scale_ref[at // depth + h], scale)
            outs[1][:, at : at + side] = (
                block * (scale / jnp.sqrt(jnp.float32(depth)))
            ).astype(BF16)
        else:
            outs[-1][:, at - width : at - width + side] = block.astype(BF16)


def project(pos, atmos, messages, surf_embed, gain, scale, w_qkv, orows, with_query, after):
    tokens, width = atmos.shape
    out_shape = (jax.ShapeDtypeStruct((tokens, 2 * width), BF16),)
    if with_query:
        out_shape = (
            jax.ShapeDtypeStruct((tokens, width), F32),
            jax.ShapeDtypeStruct((tokens, width), BF16),
        ) + out_shape
    return pl.pallas_call(
        functools.partial(project_kernel, with_query, orows),
        out_shape=out_shape,
        in_specs=[SMEM, SMEM] + [VMEM] * 7 + [pl.BlockSpec(memory_space=pl.ANY)],
        out_specs=(VMEM,) * len(out_shape),
        compiler_params=limit(20),
        cost_estimate=cost(1e12, 1e9),
        name="project",
    )(pos, scale, atmos, *messages, surf_embed, gain, w_qkv, after)


def score_part(query, lanes, per, parts):
    none = jnp.zeros_like(query)
    tops = sums = mixed = None
    for head in range(per):
        mine = jnp.where(lanes == head, query, none)
        scores = [
            lax.dot_general(mine, key, (((1,), (1,)), ((), ())), preferred_element_type=F32)
            for key, _ in parts
        ]
        top = functools.reduce(jnp.maximum, [jnp.max(s, axis=1, keepdims=True) for s in scores])
        raised = [jnp.exp(s - top) for s in scores]
        total = sum(jnp.sum(r, axis=1, keepdims=True) for r in raised)
        out = sum(
            jnp.dot(r.astype(BF16), value, preferred_element_type=F32)
            for r, (_, value) in zip(raised, parts)
        )
        if head == 0:
            shape = out.shape
            tops, sums = jnp.broadcast_to(top, shape), jnp.broadcast_to(total, shape)
            mixed = out
        else:
            tops = jnp.where(lanes == head, top, tops)
            sums = jnp.where(lanes == head, total, sums)
            mixed = jnp.where(lanes == head, out, mixed)
    return tops, sums, mixed


def near_kernel(heads, q_ref, kv0, kv1, top_ref, sum_ref, mix_ref):
    rows, width = q_ref.shape
    per = WIDE * heads // width
    lanes = iota((1, WIDE), 1) // (width // heads)

    def group(g, carry):
        part = pl.ds(pl.multiple_of(g * WIDE, WIDE), WIDE)
        there = pl.ds(pl.multiple_of(width + g * WIDE, WIDE), WIDE)
        parts = [(kv[:, part], kv[:, there]) for kv in (kv0, kv1)]
        tops, sums, mixed = score_part(q_ref[:, part], lanes, per, parts)
        top_ref[:, part] = tops
        sum_ref[:, part] = sums
        mix_ref[:, part] = mixed
        return carry

    lax.fori_loop(0, width // WIDE, group, 0)


def attend_near(query, kv0, kv1, head_count):
    shape = jax.ShapeDtypeStruct(query.shape, F32)
    return pl.pallas_call(
        functools.partial(near_kernel, head_count),
        out_shape=(shape,) * 3,
        in_specs=[VMEM] * 3,
        out_specs=(VMEM,) * 3,
        compiler_params=limit(16),
        cost_estimate=cost(1, 1),
        name="near",
    )(query, kv0, kv1)


def far_kernel(heads, message_ref, q_ref, kv_ref, top_ref, sum_ref, mix_ref, wo_ref, start_ref, gain_ref, wf_ref, next_ref, flux_ref, total):
    rows, width = q_ref.shape
    per = WIDE * heads // width
    lanes = iota((1, WIDE), 1) // (width // heads)
    penalty = jnp.where(message_ref[27:28, 0:1].astype(F32) > 0.5, 0.0, 1e30)
    total[...] = start_ref[...]

    def group(g, carry):
        part = pl.ds(pl.multiple_of(g * WIDE, WIDE), WIDE)
        there = pl.ds(pl.multiple_of(width + g * WIDE, WIDE), WIDE)
        tops, sums, mixed = score_part(
            q_ref[:, part], lanes, per, [(kv_ref[:, part], kv_ref[:, there])]
        )
        tops = tops - penalty
        top = jnp.maximum(tops, top_ref[:, part])
        here, before = jnp.exp(tops - top), jnp.exp(top_ref[:, part] - top)
        mixed = mixed * here + mix_ref[:, part] * before
        mixed = mixed / (sums * here + sum_ref[:, part] * before)
        total[...] += jnp.dot(mixed.astype(BF16), wo_ref[part], preferred_element_type=F32)
        return carry

    lax.fori_loop(0, width // WIDE, group, 0)
    after = total[...]
    next_ref[...] = after.astype(BF16)
    mean = jnp.mean(after * after, axis=1, keepdims=True)
    flux_in = (after * lax.rsqrt(mean + 1e-06) * gain_ref[...]).astype(BF16)
    flux = lax.dot_general(
        wf_ref[...], flux_in, (((1,), (1,)), ((), ())), preferred_element_type=F32
    )
    flux_ref[...] = jnp.zeros_like(flux_ref)
    flux_ref[:, 0:rows] = flux.astype(BF16)


def attend_far(message, query, kv, near, w_out, start, gain, w_flux, head_count):
    tokens, width = query.shape
    flux_count = w_flux.shape[0]
    flux_width = up_to(tokens, LANE)
    return pl.pallas_call(
        functools.partial(far_kernel, head_count),
        out_shape=(
            jax.ShapeDtypeStruct((tokens, width), BF16),
            jax.ShapeDtypeStruct((flux_count, flux_width), BF16),
        ),
        in_specs=[VMEM] * 10,
        out_specs=(VMEM, VMEM),
        scratch_shapes=[pltpu.VMEM((tokens, width), F32)],
        compiler_params=limit(20),
        cost_estimate=cost(1e12, 1e9),
        name="far",
    )(message, query, kv, *near, w_out, start, gain, w_flux)


def gate_kernel(value_ref, after_ref, out_ref):
    pass


def gate(value, after):
    anywhere = pl.BlockSpec(memory_space=pl.ANY)
    return pl.pallas_call(
        gate_kernel,
        out_shape=jax.ShapeDtypeStruct(value.shape, value.dtype),
        in_specs=[anywhere, anywhere],
        out_specs=anywhere,
        input_output_aliases={0: 0},
        compiler_params=limit(1),
        cost_estimate=cost(1, 1),
        name="gate",
    )(value, after)


def gelu(x):
    inner = x * (0.7978845608028654 + 0.035677408136300125 * (x * x))
    return 0.5 * x * (1.0 + jnp.tanh(inner))


def ocean_kernel(channels, count, pos_ref, x0, x1, x2, p0, p1, p2, f0, f1, fx, fy, c1_ref, c2_ref, next_ref, out_ref, next_hbm, zbuf, hbuf, state, masks, f_ref, w1_ref, w2_ref, w1t, turned, sem):
    copy = pltpu.make_async_copy(next_ref, next_hbm, sem)
    copy.start()
    orows, deep, width = x0.shape
    olon = out_ref.shape[2]
    nflux = f_ref.shape[1]
    fwidth = f_ref.shape[2]
    tokens = olon // SPAN
    position = pos_ref[0]
    odd = position % 2
    toward = 1 - 2 * odd
    high = 3 * deep + 3 * nflux
    hid = w1_ref.shape[0]

    f_ref[2] = f0[...]
    f_ref[2 + toward] = f1[...]
    f_ref[2 - toward] = fx[0]
    f_ref[2 - 2 * toward] = fx[1]
    f_ref[2 + 2 * toward] = fy[0]

    w1t[...] = jnp.zeros_like(w1t)
    w2_ref[...] = jnp.zeros_like(w2_ref)
    for tap in range(9):
        di, dl = tap // 3, tap % 3
        values = c1_ref[tap].astype(F32)
        at = di * high + dl * deep
        w1t[at : at + channels] = values[:channels]
        at = di * high + 3 * deep + dl * nflux
        w1t[at : at + nflux] = values[channels:]
        for k in range(2):
            at = (tap + 3 * k) * hid
            w2_ref[80 * k : 80 * k + channels, at : at + hid] = c2_ref[tap]
    w1_ref[...] = w1t[...].T.astype(BF16)

    def put_state(row, values):
        values = values.astype(BF16)
        zbuf[row, 0:deep] = pltpu.roll(values, 1, 1)
        zbuf[row, deep : 2 * deep] = values
        zbuf[row, 2 * deep : 3 * deep] = pltpu.roll(values, width - 1, 1)

    blocks = (
        (x0, p0, orows),
        (x1, p1, 2 * orows * (1 - odd)),
        (x2, p2, 2 * orows * odd),
    )
    expand = jnp.where(
        iota((LANE, SPAN * LANE), 0) == iota((LANE, SPAN * LANE), 1) // SPAN, 1.0, 0.0
    ).astype(BF16)
    flane = iota((1, fwidth), 1)
    for x_ref, p_ref, base in blocks:
        block = base // orows
        for i in range(orows):
            row = base + i
            values = x_ref[i].astype(F32)
            put_state(row, values)
            state[row] = values[0:80]
            masks[pl.ds(row, 1)] = values[channels : channels + 1][None]
            first, second = (
                p_ref[20 + b : 21 + b, i : i + 1].astype(F32)
                + p_ref[22 + b : 23 + b, i : i + 1].astype(F32)
                + p_ref[24 + b : 25 + b, i : i + 1].astype(F32)
                for b in range(2)
            )
            begin = p_ref[26:27, i : i + 1].astype(F32)
            total = None
            for d in (-1, 0, 1):
                coef = jnp.where(begin == d, first, 0.0) + jnp.where(
                    begin + 1.0 == d, second, 0.0
                )
                term = coef * f_ref[block + 1 + d].astype(F32)
                total = term if total is None else total + term
            ahead = pltpu.roll(total, tokens, 1)
            behind = pltpu.roll(total, fwidth - tokens, 1)
            total = jnp.where(flane == tokens, ahead, total)
            total = jnp.where(flane == fwidth - 1, behind, total)
            total = total.astype(BF16)
            spread = jnp.concatenate(
                [
                    jnp.dot(total[:, at : at + LANE], expand, preferred_element_type=F32)
                    for at in range(0, fwidth, LANE)
                ],
                axis=1,
            )
            at = 3 * deep
            zbuf[row, at : at + nflux] = pltpu.roll(spread, 1, 1).astype(BF16)
            zbuf[row, at + nflux : at + 2 * nflux] = spread.astype(BF16)
            zbuf[row, at + 2 * nflux : at + 3 * nflux] = pltpu.roll(spread, width - 1, 1).astype(BF16)

    def hidden_row(row, zrow, slot):
        taps = zbuf[pl.ds(zrow, 3)].reshape(3 * high, width)
        values = gelu(jnp.dot(w1_ref[...], taps, preferred_element_type=F32))
        place = position * orows + row
        keep = (place >= 0) & (place < count * orows)
        values = values * jnp.where(keep, 1.0, 0.0).astype(F32)
        values = values.astype(BF16)
        hbuf[slot, 0:hid] = pltpu.roll(values, 1, 1)
        hbuf[slot, hid : 2 * hid] = values
        hbuf[slot, 2 * hid : 3 * hid] = pltpu.roll(values, width - 1, 1)

    def pair_update(hrow, srow):
        taps = hbuf[pl.ds(hrow, 4)].reshape(4 * 3 * hid, width)
        both = jnp.dot(w2_ref[...], taps, preferred_element_type=F32)
        for k in range(2):
            state[srow + k] += masks[srow + k] * both[80 * k : 80 * k + 80]

    def first_hidden(j, carry):
        hidden_row(j - 3, j, j)
        return carry

    lax.fori_loop(0, orows + 6, first_hidden, 0, unroll=True)

    def first_state(k, carry):
        pair_update(2 * k, 2 * k + 2)
        for m in range(2):
            put_state(2 * k + 2 + m, jnp.concatenate(
                [state[2 * k + 2 + m], jnp.zeros((deep - 80, width), F32)], axis=0
            ) if deep > 80 else state[2 * k + 2 + m])
        return carry

    lax.fori_loop(0, (orows + 4) // 2, first_state, 0, unroll=True)

    def second_hidden(j, carry):
        hidden_row(j - 1, j + 2, j)
        return carry

    lax.fori_loop(0, orows + 2, second_hidden, 0, unroll=True)
    for k in range(orows // 2):
        pair_update(2 * k, 2 * k + orows)
    for i in range(orows):
        turned[:, i, :] = state[orows + i][0:channels, 0:olon]
    out_ref[...] = turned[...].astype(BF16)
    copy.wait()


def ocean(pos, xs, messages, flux, conv_first, conv_second, tokens, channels, olon, count):
    orows, deep, width = xs[0].shape
    hid = conv_second.shape[2]
    nflux, fwidth = flux[0].shape
    high = 3 * deep + 3 * nflux
    return pl.pallas_call(
        functools.partial(ocean_kernel, channels, count),
        out_shape=(
            jax.ShapeDtypeStruct((channels, orows, olon), BF16),
            jax.ShapeDtypeStruct(tokens.shape, tokens.dtype),
        ),
        in_specs=[SMEM] + [VMEM] * 13,
        out_specs=(VMEM, pl.BlockSpec(memory_space=pltpu.HBM)),
        scratch_shapes=[
            pltpu.VMEM((3 * orows, high, width), BF16),
            pltpu.VMEM((orows + 6, 3 * hid, width), BF16),
            pltpu.VMEM((3 * orows, 80, width), F32),
            pltpu.VMEM((3 * orows, 1, width), F32),
            pltpu.VMEM((5, nflux, fwidth), BF16),
            pltpu.VMEM((hid, 3 * high), BF16),
            pltpu.VMEM((160, 12 * hid), BF16),
            pltpu.VMEM((3 * high, hid), F32),
            pltpu.VMEM((channels, orows, olon), F32),
            pltpu.SemaphoreType.DMA,
        ],
        compiler_params=limit(44),
        cost_estimate=cost(2e10, 1e7),
        name="ocean",
    )(pos, *xs, *messages, *flux, conv_first, conv_second, tokens)


def local(
    atmos,
    ocean_state,
    land_mask,
    w_qkv,
    w_out,
    head_scale,
    gain_attn,
    gain_flux,
    w_flux,
    surf_embed,
    flux_start,
    flux_weight,
    surf_start,
    surf_weight,
    conv_first,
    conv_second,
):
    position = lax.axis_index("lat")
    count = lax.axis_size("lat")
    channels, orows, olon = ocean_state.shape
    width = atmos.shape[1]
    head_count = head_scale.shape[0]
    pos = position.reshape(1).astype(jnp.int32)

    own = surface_message(pos, ocean_state, surf_start, surf_weight, flux_start, flux_weight)
    partner = swap_in_chip(own)
    far = swap_across(jnp.stack([own, partner]))
    cross, cross2 = far[0], far[1]
    atmos_cross = swap_across(atmos)

    gain_a = gain_attn.reshape(1, width)
    start, query, kv_own = project(
        pos, atmos, (own, partner, cross), surf_embed, gain_a, head_scale, w_qkv, orows, True, own
    )
    kv_partner = swap_in_chip(kv_own)
    xs_own = relayout(ocean_state, land_mask, query)
    near = attend_near(query, kv_own, kv_partner, head_count)
    (kv_cross,) = project(
        pos,
        atmos_cross,
        (cross, own, cross2),
        surf_embed,
        gain_a,
        head_scale,
        w_qkv,
        orows,
        False,
        near[0],
    )
    xs_own = gate(xs_own, query)
    xs_partner = swap_in_chip(xs_own)
    xs_cross = swap_across(xs_own)
    atmos_next, flux = attend_far(
        cross,
        query,
        kv_cross,
        near,
        w_out,
        start,
        gain_flux.reshape(1, width),
        w_flux.T,
        head_count,
    )
    flux_partner = swap_in_chip(flux)
    flux_far = swap_across(jnp.stack([flux, flux_partner]))
    flux_far2 = swap_in_chip(flux_far)
    ocean_next, atmos_next = ocean(
        pos,
        (xs_own, xs_partner, xs_cross),
        (own, partner, cross),
        (flux, flux_partner, flux_far, flux_far2),
        conv_first.transpose(0, 2, 1),
        conv_second,
        atmos_next,
        channels,
        olon,
        count,
    )
    return atmos_next, ocean_next


def solution(mesh):
    in_specs = (
        P(("ens", "lat"), None),
        P(None, ("ens", "lat"), None),
        P("lat", None),
        P(),
        P(),
        P(),
        P(),
        P(),
        P(),
        P(),
        P("lat"),
        P("lat", None),
        P("lat"),
        P("lat", None),
        P(),
        P(),
    )
    out_specs = (P(("ens", "lat"), None), P(None, ("ens", "lat"), None))
    return jax.shard_map(local, mesh=mesh, in_specs=in_specs, out_specs=out_specs, check_vma=False)
```

```python
import functools

import jax
import jax.numpy as jnp
from jax import lax
from jax.experimental import pallas as pl
from jax.experimental.pallas import tpu as pltpu
from jax.sharding import PartitionSpec as P

LEVELS = 19
VARS = 4
SPAN = 4
PSIDE = 1024
WIDE = 256
LANE = 128
F32 = jnp.float32
BF16 = jnp.bfloat16
VMEM = pl.BlockSpec(memory_space=pltpu.VMEM)
SMEM = pl.BlockSpec(memory_space=pltpu.SMEM)


def limit(mebibytes):
    return pltpu.CompilerParams(vmem_limit_bytes=mebibytes * 2**20)


def cost(flops, size):
    return pl.CostEstimate(flops=int(flops), bytes_accessed=int(size), transcendentals=0)


def up_to(value, unit):
    return (value + unit - 1) // unit * unit


def iota(shape, axis):
    return lax.broadcasted_iota(jnp.int32, shape, axis)


def swap_in_chip(block):
    count = lax.axis_size("lat")
    return lax.ppermute(block, "lat", [(i, i ^ 1) for i in range(count)])


def swap_across(block):
    count = lax.axis_size("lat")
    pairs = []
    for i in range(1, count - 1, 2):
        pairs += [(i, i + 1), (i + 1, i)]
    return lax.ppermute(block, "lat", pairs)


def split3(values):
    high = values.astype(BF16)
    rest = values - high.astype(F32)
    middle = rest.astype(BF16)
    low = (rest - middle.astype(F32)).astype(BF16)
    return high, middle, low


def surface_kernel(pos_ref, small_ref, ocean_ref, out_ref, tile, *refs):
    fields, sems = refs
    orows, olon = fields.shape[1:]
    copies = [
        pltpu.make_async_copy(ocean_ref.at[v * LEVELS], fields.at[v], sems.at[v])
        for v in range(VARS)
    ]
    for copy in copies:
        copy.start()
    for copy in copies:
        copy.wait()
    wide = SPAN * LANE
    parts = jnp.concatenate([fields[v].astype(F32) for v in range(VARS)], axis=0).astype(BF16)
    gather = jnp.where(iota((wide, LANE), 0) // SPAN == iota((wide, LANE), 1), 1.0 / SPAN, 0.0)
    gather = gather.astype(BF16)
    tile[...] = jnp.zeros_like(tile)
    for at in range(0, olon, wide):
        size = min(wide, olon - at)
        tile[0:16, at // SPAN : at // SPAN + LANE] = jnp.dot(
            parts[:, at : at + size], gather[:size], preferred_element_type=F32
        )
    lanes = small_ref.shape[1]
    weights = lanes - 1 - orows - 2 * orows
    small = small_ref[...]
    for index, piece in enumerate(split3(small[:, 0:weights])):
        tile[16 + index : 17 + index, 0:weights] = piece.astype(F32)
    position = pos_ref[0].astype(F32)
    for band in range(2):
        at = weights + band * orows
        for index, piece in enumerate(split3(small[:, at : at + orows])):
            row = 20 + 2 * index + band
            tile[row : row + 1, 0:orows] = piece.astype(F32)
    at = weights + 2 * orows
    tile[26:27, 0:orows] = small[:, at : at + orows] - position
    tile[19:20, 0:1] = small[:, at + orows : lanes] - position * orows
    tile[27:28, 0:LANE] = jnp.ones((1, LANE), F32)
    out_ref[...] = tile[...].astype(BF16)


def surface_message(pos, ocean_state, surf_start, surf_weight, flux_start, flux_weight):
    channels, orows, olon = ocean_state.shape
    width = up_to(olon // SPAN, LANE)
    bands = flux_weight.T
    pieces = [surf_weight, bands[0:1], bands[1:2]]
    pieces += [flux_start.astype(F32).reshape(1, -1), surf_start.astype(F32).reshape(1, -1)]
    lanes = sum(piece.shape[1] for piece in pieces)
    small, at = None, 0
    for piece in pieces:
        size = piece.shape[1]
        padded = jnp.pad(piece, ((0, 0), (at, lanes - at - size)))
        small = padded if small is None else small + padded
        at += size
    return pl.pallas_call(
        surface_kernel,
        out_shape=jax.ShapeDtypeStruct((32, width), BF16),
        in_specs=[SMEM, VMEM, pl.BlockSpec(memory_space=pl.ANY)],
        out_specs=VMEM,
        scratch_shapes=[
            pltpu.VMEM((32, width), F32),
            pltpu.VMEM((VARS, orows, olon), BF16),
            pltpu.SemaphoreType.DMA((VARS,)),
        ],
        compiler_params=limit(8),
        cost_estimate=cost(1e12, 1e9),
        name="surface",
    )(pos, small, ocean_state)


def relayout_kernel(ocean_ref, mask_ref, after_ref, out_ref, wide, row_ref):
    channels, orows, olon = ocean_ref.shape
    width = out_ref.shape[2]
    wide[...] = ocean_ref[...].astype(F32)
    row_ref[...] = jnp.zeros_like(row_ref)
    pad = width - olon
    lanes = iota((1, width), 1)
    for row in range(orows):
        row_ref[0:channels, 0:olon] = wide[:, row, :]
        row_ref[channels : channels + 1, 0:olon] = mask_ref[row : row + 1, :].astype(F32)
        values = row_ref[...]
        ahead = pltpu.roll(values, olon, 1)
        behind = pltpu.roll(values, pad, 1)
        values = jnp.where((lanes >= olon) & (lanes < olon + SPAN), ahead, values)
        values = jnp.where(lanes >= width - SPAN, behind, values)
        out_ref[row] = values.astype(BF16)


def relayout(ocean_state, land_mask, after):
    channels, orows, olon = ocean_state.shape
    width = up_to(olon + 2 * SPAN, LANE)
    deep = up_to(channels + 1, 16)
    return pl.pallas_call(
        relayout_kernel,
        out_shape=jax.ShapeDtypeStruct((orows, deep, width), BF16),
        in_specs=[VMEM, VMEM, pl.BlockSpec(memory_space=pl.ANY)],
        out_specs=VMEM,
        scratch_shapes=[pltpu.VMEM((channels, orows, olon), F32), pltpu.VMEM((deep, width), F32)],
        compiler_params=limit(16),
        cost_estimate=cost(1e12, 1e9),
        name="relayout",
    )(ocean_state, land_mask, after)


def head_norm(block):
    side = 256
    ones = jnp.where(iota((side, side), 0) // 64 == iota((side, side), 1) // 64, 1.0, 0.0)
    ones = ones.astype(BF16)
    out = []
    for at in range(0, block.shape[1], side):
        part = block[:, at : at + side]
        square = part * part
        high = square.astype(BF16)
        low = (square - high.astype(F32)).astype(BF16)
        total = jnp.dot(high, ones, preferred_element_type=F32)
        total = total + jnp.dot(low, ones, preferred_element_type=F32)
        out.append(part * lax.rsqrt(total * (1.0 / 64) + 1e-06))
    return jnp.concatenate(out, axis=1)


def tokens_start(atmos, embed, sfields, places, params, orows):
    starts = params[19:20, 0:1].astype(F32)
    weights = (
        params[16:17].astype(F32) + params[17:18].astype(F32) + params[18:19].astype(F32)
    )[:, 0:LANE]
    rows = iota((16, LANE), 0) % orows
    lanes = iota((16, LANE), 1)
    total = None
    for block, fields in zip(places, sfields):
        place = rows + block * orows - starts.astype(jnp.int32)
        coef = jnp.sum(jnp.where(lanes == place, weights, 0.0), axis=1, keepdims=True)
        term = coef * fields[0:16].astype(F32)
        total = term if total is None else total + term
    a = split3(total)
    rep = jnp.concatenate(
        [jnp.broadcast_to(embed[v : v + 1], (orows, embed.shape[1])) for v in range(VARS)], axis=0
    )
    b = split3(rep)
    left = jnp.concatenate([a[0], a[0], a[0], a[1], a[1], a[2]], axis=0)
    right = jnp.concatenate([b[0], b[1], b[2], b[0], b[1], b[0]], axis=0)
    added = lax.dot_general(left, right, (((0,), (0,)), ((), ())), preferred_element_type=F32)
    return atmos.astype(F32) + added[: atmos.shape[0]]


def project_kernel(with_query, orows, pos_ref, scale_ref, atmos_ref, m0, m1, m2, embed_ref, gain_ref, w_ref, after_ref, *refs):
    outs = refs
    width, columns = w_ref.shape
    depth = width // scale_ref.shape[0]
    side = min(PSIDE, width)
    toward = 1 - 2 * (pos_ref[0] % 2)
    start = tokens_start(
        atmos_ref[...],
        embed_ref[...],
        (m0[...], m1[...], m2[...]),
        (0, toward, -toward),
        m0[...],
        orows,
    )
    mean = jnp.mean(start * start, axis=1, keepdims=True)
    normed = (start * lax.rsqrt(mean + 1e-06) * gain_ref[...]).astype(BF16)
    if with_query:
        outs[0][...] = start
    for at in range(0 if with_query else width, columns, side):
        block = jnp.dot(normed, w_ref[:, at : at + side], preferred_element_type=F32)
        if at < 2 * width:
            block = head_norm(block)
        if at < width:
            heads = iota((1, side), 1) // depth
            scale = jnp.zeros((1, side), F32)
            for h in range(side // depth):
                scale = jnp.where(heads == h, scale_ref[at // depth + h], scale)
            outs[1][:, at : at + side] = (
                block * (scale / jnp.sqrt(jnp.float32(depth)))
            ).astype(BF16)
        else:
            outs[-1][:, at - width : at - width + side] = block.astype(BF16)


def project(pos, atmos, messages, surf_embed, gain, scale, w_qkv, orows, with_query, after):
    tokens, width = atmos.shape
    out_shape = (jax.ShapeDtypeStruct((tokens, 2 * width), BF16),)
    if with_query:
        out_shape = (
            jax.ShapeDtypeStruct((tokens, width), F32),
            jax.ShapeDtypeStruct((tokens, width), BF16),
        ) + out_shape
    return pl.pallas_call(
        functools.partial(project_kernel, with_query, orows),
        out_shape=out_shape,
        in_specs=[SMEM, SMEM] + [VMEM] * 7 + [pl.BlockSpec(memory_space=pl.ANY)],
        out_specs=(VMEM,) * len(out_shape),
        compiler_params=limit(20),
        cost_estimate=cost(1e12, 1e9),
        name="project",
    )(pos, scale, atmos, *messages, surf_embed, gain, w_qkv, after)


def score_part(query, lanes, per, parts):
    none = jnp.zeros_like(query)
    tops = sums = mixed = None
    for head in range(per):
        mine = jnp.where(lanes == head, query, none)
        scores = [
            lax.dot_general(mine, key, (((1,), (1,)), ((), ())), preferred_element_type=F32)
            for key, _ in parts
        ]
        top = functools.reduce(jnp.maximum, [jnp.max(s, axis=1, keepdims=True) for s in scores])
        raised = [jnp.exp(s - top) for s in scores]
        total = sum(jnp.sum(r, axis=1, keepdims=True) for r in raised)
        out = sum(
            jnp.dot(r.astype(BF16), value, preferred_element_type=F32)
            for r, (_, value) in zip(raised, parts)
        )
        if head == 0:
            shape = out.shape
            tops, sums = jnp.broadcast_to(top, shape), jnp.broadcast_to(total, shape)
            mixed = out
        else:
            tops = jnp.where(lanes == head, top, tops)
            sums = jnp.where(lanes == head, total, sums)
            mixed = jnp.where(lanes == head, out, mixed)
    return tops, sums, mixed


def near_kernel(heads, q_ref, kv0, kv1, top_ref, sum_ref, mix_ref):
    rows, width = q_ref.shape
    per = WIDE * heads // width
    lanes = iota((1, WIDE), 1) // (width // heads)

    def group(g, carry):
        part = pl.ds(pl.multiple_of(g * WIDE, WIDE), WIDE)
        there = pl.ds(pl.multiple_of(width + g * WIDE, WIDE), WIDE)
        parts = [(kv[:, part], kv[:, there]) for kv in (kv0, kv1)]
        tops, sums, mixed = score_part(q_ref[:, part], lanes, per, parts)
        top_ref[:, part] = tops
        sum_ref[:, part] = sums
        mix_ref[:, part] = mixed
        return carry

    lax.fori_loop(0, width // WIDE, group, 0)


def attend_near(query, kv0, kv1, head_count):
    shape = jax.ShapeDtypeStruct(query.shape, F32)
    return pl.pallas_call(
        functools.partial(near_kernel, head_count),
        out_shape=(shape,) * 3,
        in_specs=[VMEM] * 3,
        out_specs=(VMEM,) * 3,
        compiler_params=limit(16),
        cost_estimate=cost(1, 1),
        name="near",
    )(query, kv0, kv1)


def far_kernel(heads, message_ref, q_ref, kv_ref, top_ref, sum_ref, mix_ref, wo_ref, start_ref, gain_ref, wf_ref, next_ref, flux_ref, total):
    rows, width = q_ref.shape
    per = WIDE * heads // width
    lanes = iota((1, WIDE), 1) // (width // heads)
    penalty = jnp.where(message_ref[27:28, 0:1].astype(F32) > 0.5, 0.0, 1e30)
    total[...] = start_ref[...]

    def group(g, carry):
        part = pl.ds(pl.multiple_of(g * WIDE, WIDE), WIDE)
        there = pl.ds(pl.multiple_of(width + g * WIDE, WIDE), WIDE)
        tops, sums, mixed = score_part(
            q_ref[:, part], lanes, per, [(kv_ref[:, part], kv_ref[:, there])]
        )
        tops = tops - penalty
        top = jnp.maximum(tops, top_ref[:, part])
        here, before = jnp.exp(tops - top), jnp.exp(top_ref[:, part] - top)
        mixed = mixed * here + mix_ref[:, part] * before
        mixed = mixed / (sums * here + sum_ref[:, part] * before)
        total[...] += jnp.dot(mixed.astype(BF16), wo_ref[part], preferred_element_type=F32)
        return carry

    lax.fori_loop(0, width // WIDE, group, 0)
    after = total[...]
    next_ref[...] = after.astype(BF16)
    mean = jnp.mean(after * after, axis=1, keepdims=True)
    flux_in = (after * lax.rsqrt(mean + 1e-06) * gain_ref[...]).astype(BF16)
    flux = lax.dot_general(
        wf_ref[...], flux_in, (((1,), (1,)), ((), ())), preferred_element_type=F32
    )
    flux_ref[...] = jnp.zeros_like(flux_ref)
    flux_ref[:, 0:rows] = flux.astype(BF16)


def attend_far(message, query, kv, near, w_out, start, gain, w_flux, head_count):
    tokens, width = query.shape
    flux_count = w_flux.shape[0]
    flux_width = up_to(tokens, LANE)
    return pl.pallas_call(
        functools.partial(far_kernel, head_count),
        out_shape=(
            jax.ShapeDtypeStruct((tokens, width), BF16),
            jax.ShapeDtypeStruct((flux_count, flux_width), BF16),
        ),
        in_specs=[VMEM] * 10,
        out_specs=(VMEM, VMEM),
        scratch_shapes=[pltpu.VMEM((tokens, width), F32)],
        compiler_params=limit(20),
        cost_estimate=cost(1e12, 1e9),
        name="far",
    )(message, query, kv, *near, w_out, start, gain, w_flux)


def gate_kernel(value_ref, after_ref, out_ref):
    pass


def gate(value, after):
    anywhere = pl.BlockSpec(memory_space=pl.ANY)
    return pl.pallas_call(
        gate_kernel,
        out_shape=jax.ShapeDtypeStruct(value.shape, value.dtype),
        in_specs=[anywhere, anywhere],
        out_specs=anywhere,
        input_output_aliases={0: 0},
        compiler_params=limit(1),
        cost_estimate=cost(1, 1),
        name="gate",
    )(value, after)


def gelu(x):
    inner = x * (0.7978845608028654 + 0.035677408136300125 * (x * x))
    return 0.5 * x * (1.0 + jnp.tanh(inner))


def ocean_kernel(channels, count, pos_ref, x0, x1, x2, p0, p1, p2, f0, f1, fx, fy, c1_ref, c2_ref, next_ref, out_ref, next_hbm, zbuf, hbuf, state, masks, f_ref, w1_ref, w2_ref, w1t, turned, ftot, sem):
    copy = pltpu.make_async_copy(next_ref, next_hbm, sem)
    copy.start()
    orows, deep, width = x0.shape
    olon = out_ref.shape[2]
    nflux = f_ref.shape[1]
    fwidth = f_ref.shape[2]
    tokens = olon // SPAN
    position = pos_ref[0]
    odd = position % 2
    toward = 1 - 2 * odd
    high = 3 * deep + 3 * nflux
    hid = w1_ref.shape[0]

    f_ref[2] = f0[...]
    f_ref[2 + toward] = f1[...]
    f_ref[2 - toward] = fx[0]
    f_ref[2 - 2 * toward] = fx[1]
    f_ref[2 + 2 * toward] = fy[0]

    w1t[...] = jnp.zeros_like(w1t)
    w2_ref[...] = jnp.zeros_like(w2_ref)
    for tap in range(9):
        di, dl = tap // 3, tap % 3
        values = c1_ref[tap].astype(F32)
        at = di * high + dl * deep
        w1t[at : at + channels] = values[:channels]
        at = di * high + 3 * deep + dl * nflux
        w1t[at : at + nflux] = values[channels:]
        for k in range(2):
            at = (tap + 3 * k) * hid
            w2_ref[80 * k : 80 * k + channels, at : at + hid] = c2_ref[tap]
    w1_ref[...] = w1t[...].T.astype(BF16)

    def put_state(row, values):
        values = values.astype(BF16)
        zbuf[row, 0:deep] = pltpu.roll(values, 1, 1)
        zbuf[row, deep : 2 * deep] = values
        zbuf[row, 2 * deep : 3 * deep] = pltpu.roll(values, width - 1, 1)

    blocks = (
        (x0, p0, orows),
        (x1, p1, 2 * orows * (1 - odd)),
        (x2, p2, 2 * orows * odd),
    )
    expand = jnp.where(
        iota((LANE, SPAN * LANE), 0) == iota((LANE, SPAN * LANE), 1) // SPAN, 1.0, 0.0
    ).astype(BF16)
    flane = iota((1, fwidth), 1)
    for x_ref, p_ref, base in blocks:
        block = base // orows
        for i in range(orows):
            row = base + i
            values = x_ref[i].astype(F32)
            put_state(row, values)
            state[row] = values[0:80]
            masks[pl.ds(row, 1)] = values[channels : channels + 1][None]
            first, second = (
                p_ref[20 + b : 21 + b, i : i + 1].astype(F32)
                + p_ref[22 + b : 23 + b, i : i + 1].astype(F32)
                + p_ref[24 + b : 25 + b, i : i + 1].astype(F32)
                for b in range(2)
            )
            begin = p_ref[26:27, i : i + 1].astype(F32)
            total = None
            for d in (-1, 0, 1):
                coef = jnp.where(begin == d, first, 0.0) + jnp.where(
                    begin + 1.0 == d, second, 0.0
                )
                term = coef * f_ref[block + 1 + d].astype(F32)
                total = term if total is None else total + term
            ahead = pltpu.roll(total, tokens, 1)
            behind = pltpu.roll(total, fwidth - tokens, 1)
            total = jnp.where(flane == tokens, ahead, total)
            total = jnp.where(flane == fwidth - 1, behind, total)
            ftot[row] = total.astype(BF16)
    every = ftot[...].reshape(3 * orows * nflux, fwidth)
    spread = jnp.concatenate(
        [
            jnp.dot(every[:, at : at + LANE], expand, preferred_element_type=F32)
            for at in range(0, fwidth, LANE)
        ],
        axis=1,
    ).astype(BF16)
    left, right = pltpu.roll(spread, 1, 1), pltpu.roll(spread, width - 1, 1)
    for row in range(3 * orows):
        mine = slice(row * nflux, (row + 1) * nflux)
        at = 3 * deep
        zbuf[row, at : at + nflux] = left[mine]
        zbuf[row, at + nflux : at + 2 * nflux] = spread[mine]
        zbuf[row, at + 2 * nflux : at + 3 * nflux] = right[mine]

    def hidden_row(row, zrow, slot):
        taps = zbuf[pl.ds(zrow, 3)].reshape(3 * high, width)
        values = gelu(jnp.dot(w1_ref[...], taps, preferred_element_type=F32))
        place = position * orows + row
        keep = (place >= 0) & (place < count * orows)
        values = values * jnp.where(keep, 1.0, 0.0).astype(F32)
        values = values.astype(BF16)
        hbuf[slot, 0:hid] = pltpu.roll(values, 1, 1)
        hbuf[slot, hid : 2 * hid] = values
        hbuf[slot, 2 * hid : 3 * hid] = pltpu.roll(values, width - 1, 1)

    def pair_update(hrow, srow):
        taps = hbuf[pl.ds(hrow, 4)].reshape(4 * 3 * hid, width)
        both = jnp.dot(w2_ref[...], taps, preferred_element_type=F32)
        for k in range(2):
            state[srow + k] += masks[srow + k] * both[80 * k : 80 * k + 80]

    def first_hidden(j, carry):
        hidden_row(j - 3, j, j)
        return carry

    lax.fori_loop(0, orows + 6, first_hidden, 0, unroll=True)

    def first_state(k, carry):
        pair_update(2 * k, 2 * k + 2)
        for m in range(2):
            put_state(2 * k + 2 + m, jnp.concatenate(
                [state[2 * k + 2 + m], jnp.zeros((deep - 80, width), F32)], axis=0
            ) if deep > 80 else state[2 * k + 2 + m])
        return carry

    lax.fori_loop(0, (orows + 4) // 2, first_state, 0, unroll=True)

    def second_hidden(j, carry):
        hidden_row(j - 1, j + 2, j)
        return carry

    lax.fori_loop(0, orows + 2, second_hidden, 0, unroll=True)
    for k in range(orows // 2):
        pair_update(2 * k, 2 * k + orows)
    for i in range(orows):
        turned[:, i, :] = state[orows + i][0:channels, 0:olon]
    out_ref[...] = turned[...].astype(BF16)
    copy.wait()


def ocean(pos, xs, messages, flux, conv_first, conv_second, tokens, channels, olon, count):
    orows, deep, width = xs[0].shape
    hid = conv_second.shape[2]
    nflux, fwidth = flux[0].shape
    high = 3 * deep + 3 * nflux
    return pl.pallas_call(
        functools.partial(ocean_kernel, channels, count),
        out_shape=(
            jax.ShapeDtypeStruct((channels, orows, olon), BF16),
            jax.ShapeDtypeStruct(tokens.shape, tokens.dtype),
        ),
        in_specs=[SMEM] + [VMEM] * 13,
        out_specs=(VMEM, pl.BlockSpec(memory_space=pltpu.HBM)),
        scratch_shapes=[
            pltpu.VMEM((3 * orows, high, width), BF16),
            pltpu.VMEM((orows + 6, 3 * hid, width), BF16),
            pltpu.VMEM((3 * orows, 80, width), F32),
            pltpu.VMEM((3 * orows, 1, width), F32),
            pltpu.VMEM((5, nflux, fwidth), BF16),
            pltpu.VMEM((hid, 3 * high), BF16),
            pltpu.VMEM((160, 12 * hid), BF16),
            pltpu.VMEM((3 * high, hid), F32),
            pltpu.VMEM((channels, orows, olon), F32),
            pltpu.VMEM((3 * orows, nflux, fwidth), BF16),
            pltpu.SemaphoreType.DMA,
        ],
        compiler_params=limit(44),
        cost_estimate=cost(2e10, 1e7),
        name="ocean",
    )(pos, *xs, *messages, *flux, conv_first, conv_second, tokens)


def local(
    atmos,
    ocean_state,
    land_mask,
    w_qkv,
    w_out,
    head_scale,
    gain_attn,
    gain_flux,
    w_flux,
    surf_embed,
    flux_start,
    flux_weight,
    surf_start,
    surf_weight,
    conv_first,
    conv_second,
):
    position = lax.axis_index("lat")
    count = lax.axis_size("lat")
    channels, orows, olon = ocean_state.shape
    width = atmos.shape[1]
    head_count = head_scale.shape[0]
    pos = position.reshape(1).astype(jnp.int32)

    own = surface_message(pos, ocean_state, surf_start, surf_weight, flux_start, flux_weight)
    partner = swap_in_chip(own)
    far = swap_across(jnp.stack([own, partner]))
    cross, cross2 = far[0], far[1]
    atmos_cross = swap_across(atmos)

    gain_a = gain_attn.reshape(1, width)
    start, query, kv_own = project(
        pos, atmos, (own, partner, cross), surf_embed, gain_a, head_scale, w_qkv, orows, True, own
    )
    kv_partner = swap_in_chip(kv_own)
    xs_own = relayout(ocean_state, land_mask, query)
    near = attend_near(query, kv_own, kv_partner, head_count)
    (kv_cross,) = project(
        pos,
        atmos_cross,
        (cross, own, cross2),
        surf_embed,
        gain_a,
        head_scale,
        w_qkv,
        orows,
        False,
        near[0],
    )
    xs_own = gate(xs_own, query)
    xs_partner = swap_in_chip(xs_own)
    xs_cross = swap_across(xs_own)
    atmos_next, flux = attend_far(
        cross,
        query,
        kv_cross,
        near,
        w_out,
        start,
        gain_flux.reshape(1, width),
        w_flux.T,
        head_count,
    )
    flux_partner = swap_in_chip(flux)
    flux_far = swap_across(jnp.stack([flux, flux_partner]))
    flux_far2 = swap_in_chip(flux_far)
    ocean_next, atmos_next = ocean(
        pos,
        (xs_own, xs_partner, xs_cross),
        (own, partner, cross),
        (flux, flux_partner, flux_far, flux_far2),
        conv_first.transpose(0, 2, 1),
        conv_second,
        atmos_next,
        channels,
        olon,
        count,
    )
    return atmos_next, ocean_next


def solution(mesh):
    in_specs = (
        P(("ens", "lat"), None),
        P(None, ("ens", "lat"), None),
        P("lat", None),
        P(),
        P(),
        P(),
        P(),
        P(),
        P(),
        P(),
        P("lat"),
        P("lat", None),
        P("lat"),
        P("lat", None),
        P(),
        P(),
    )
    out_specs = (P(("ens", "lat"), None), P(None, ("ens", "lat"), None))
    return jax.shard_map(local, mesh=mesh, in_specs=in_specs, out_specs=out_specs, check_vma=False)
```
